512 devices in a mesh: rows: 128 (over z, y, core), grp: 4 (over x).
Axes of the slice: x: 4, y: 8, z: 8, core: 2. Of those that a mesh axis runs over, the one named last changes fastest.
Arguments:
- values: bfloat16 [2048, 64, 256], P(('rows', 'grp'))
- pattern: int32 [2048, 4], P(('rows', 'grp')), may hold values from 0 to 15, as said below
- targets: float32 [131072], P(('rows', 'grp')), may hold values from -6 to 6
- root_weights: float32 [131072], P(('rows', 'grp')), may hold values from 0.25 to 4
Outputs:
- solution: float32 [1024], replicated
- fitted: float32 [131072], P(('rows', 'grp'))
The draws below stay inside these ranges and needn't reach their ends.
Inputs may be any that keep to these rules, and one draw needn't show every extreme that they name: `pattern`: each tile's 4 entries name distinct column blocks.
All inputs are finite; a program needn't handle non-finite values.
Results may differ from the reference program's by a relative error of at most 0.00035.
Values sent between devices are 32-bit elements; how exact they have to be, the bound alone decides.
A program may use at most 128 MiB of HBM per device.

```python
import math
import jax
import jax.numpy as jnp
from jax import lax

NC = 1024
BLK = 64
KB = 4
ITERS = 2
NB = 16
TILES = 2048
ROWS = 131072


def block_pattern(key):
    scores = jax.random.randint(key, (TILES, NB), 0, 1 << 20) * NB + jnp.arange(NB, dtype=jnp.int32)[None, :]
    return lax.top_k(scores, KB)[1].astype(jnp.int32)


def draw_pattern(key, part):
    return block_pattern(key)


def draw_root_weights(key, part):
    tile_pattern = block_pattern(key)
    key = jax.random.fold_in(key, 11)
    level_key, noise_key = jax.random.split(key)
    levels = jax.random.uniform(level_key, (NB,), jnp.float32, -0.5, 0.5)
    per_tile = jnp.sum(levels[tile_pattern], axis=1)
    noise = jax.random.uniform(noise_key, (TILES, BLK), jnp.float32, -0.3, 0.3)
    return jnp.exp(0.5 * per_tile[:, None] + noise).reshape(TILES * BLK)


def draw_values(key, part):
    key = jax.random.fold_in(key, 7)
    base_key, scale_key, common_key = jax.random.split(key, 3)
    rising = 0.5 + jnp.arange(TILES, dtype=jnp.float32) / TILES
    own = jnp.clip(jax.random.normal(base_key, (TILES, BLK, KB * BLK), jnp.float32), -4.0, 4.0)
    common = jnp.clip(jax.random.normal(common_key, (TILES, BLK), jnp.float32), -4.0, 4.0)
    row_scale = jnp.exp(jax.random.uniform(scale_key, (TILES, BLK), jnp.float32, -0.7, 0.7))
    base = 0.6 * own + 0.8 * common[:, :, None]
    scaled = base * (rising[:, None] * row_scale)[:, :, None] / math.sqrt(KB * BLK)
    return scaled.astype(jnp.bfloat16)


def shard_levels(stream_key, extent, cuts, least, largest):
    def one(position, shards_of):
        heights = jax.random.uniform(jax.random.fold_in(jax.random.fold_in(stream_key, 6), position), (shards_of,), jnp.float32, least / len(cuts), largest / len(cuts))
        return jnp.repeat(jnp.exp(heights), extent[position] // shards_of).reshape((-1,) + (1,) * (len(extent) - position - 1))

    loudness = one(*cuts[0])
    for cut in cuts[1:]:
        loudness = loudness * one(*cut)
    return loudness


def scatter_about(rng, extent, scale, reach, cuts=(), kind=jnp.bfloat16):
    result = scale * jax.random.normal(rng, extent, jnp.float32)
    if cuts:
        result = result * shard_levels(rng, extent, cuts, -0.22, 0.18)
    return jnp.clip(result, -reach, reach).astype(kind)


def setup_inputs(seed: int = 0) -> dict:
    key_list = jax.random.split(jax.random.key(seed), 5)
    values = draw_values(jax.random.fold_in(key_list[4], 71), 0)
    pattern = draw_pattern(jax.random.fold_in(key_list[4], 71), 0)
    targets = scatter_about(key_list[2], (ROWS,), 1.0, 6.0, ((0, 512),), jnp.float32)
    root_weights = draw_root_weights(jax.random.fold_in(key_list[4], 71), 0)
    return dict(values=values, pattern=pattern, targets=targets, root_weights=root_weights)


PRECISE = lax.Precision.HIGHEST

def tile_groups(values, pattern):
    tile_count = values.shape[0]
    group_size = 64 if tile_count % 64 == 0 else tile_count
    grouped = values.reshape(tile_count // group_size, group_size, BLK, KB, BLK)
    patterns = pattern.reshape(tile_count // group_size, group_size, KB)
    return (grouped, patterns)

def gram_matrix(grouped, patterns):

    def accumulate(running, element):
        tile_vals, tile_pat = element
        tile_vals = tile_vals.astype(jnp.float32)
        products = jnp.einsum('trai,trbj->tabij', tile_vals, tile_vals, precision=PRECISE)
        running = running.at[tile_pat[:, :, None], :, tile_pat[:, None, :], :].add(products)
        return (running, None)
    initial = jnp.zeros((NB, BLK, NB, BLK), jnp.float32)
    running, ignored = lax.scan(accumulate, initial, (grouped, patterns))
    return running.reshape(NC, NC)

def forward(grouped, patterns, vector):
    lookup_table = vector.reshape(NB, BLK)

    def apply_group(element):
        tile_vals, tile_pat = element
        picked = lookup_table[tile_pat]
        return jnp.einsum('trkj,tkj->tr', tile_vals.astype(jnp.float32), picked, precision=PRECISE)
    return lax.map(apply_group, (grouped, patterns)).reshape(-1)

def backward(grouped, patterns, row_vector):
    row_parts = row_vector.reshape(grouped.shape[0], grouped.shape[1], BLK)

    def accumulate(running, element):
        tile_vals, tile_pat, row_part = element
        terms = jnp.einsum('trkj,tr->tkj', tile_vals.astype(jnp.float32), row_part, precision=PRECISE)
        return (running.at[tile_pat].add(terms), None)
    initial = jnp.zeros((NB, BLK), jnp.float32)
    running, ignored = lax.scan(accumulate, initial, (grouped, patterns, row_parts))
    return running.reshape(-1)

def solve_lower(lower_factor, vector):
    return jax.scipy.linalg.solve_triangular(lower_factor, vector, lower=True)

def solve_upper(lower_factor, vector):
    return jax.scipy.linalg.solve_triangular(lower_factor, vector, lower=True, trans=1)

def reference(values, pattern, targets, root_weights):
    grouped, patterns = tile_groups(values, pattern)
    gram_total = gram_matrix(grouped, patterns)
    ridge_value = targets.shape[0] / (2.0 * NC)
    root_ridge = math.sqrt(ridge_value)
    lower_factor = jnp.linalg.cholesky(gram_total + ridge_value * jnp.eye(NC, dtype=jnp.float32))
    scaled = root_weights * targets
    beta_norm = jnp.sqrt(jnp.sum(scaled * scaled))
    u_rows = scaled / beta_norm
    u_extra = jnp.zeros((NC,), jnp.float32)
    back_vec = backward(grouped, patterns, root_weights * u_rows) + root_ridge * u_extra
    raw_right = solve_lower(lower_factor, back_vec)
    alpha_norm = jnp.sqrt(jnp.sum(raw_right * raw_right))
    right_vec = raw_right / alpha_norm
    search_dir = right_vec
    phi_bar = beta_norm
    rho_bar = alpha_norm
    iterate = jnp.zeros((NC,), jnp.float32)
    for iteration in range(ITERS):
        lifted = solve_upper(lower_factor, right_vec)
        p_rows = root_weights * forward(grouped, patterns, lifted) - alpha_norm * u_rows
        p_extra = root_ridge * lifted - alpha_norm * u_extra
        beta_norm = jnp.sqrt(jnp.sum(p_rows * p_rows) + jnp.sum(p_extra * p_extra))
        u_rows = p_rows / beta_norm
        u_extra = p_extra / beta_norm
        rho_value = jnp.sqrt(rho_bar * rho_bar + beta_norm * beta_norm)
        cosine = rho_bar / rho_value
        sine_value = beta_norm / rho_value
        phi_value = cosine * phi_bar
        phi_bar = sine_value * phi_bar
        iterate = iterate + phi_value / rho_value * search_dir
        if iteration + 1 < ITERS:
            back_vec = backward(grouped, patterns, root_weights * u_rows) + root_ridge * u_extra
            raw_right = solve_lower(lower_factor, back_vec) - beta_norm * right_vec
            alpha_norm = jnp.sqrt(jnp.sum(raw_right * raw_right))
            right_vec = raw_right / alpha_norm
            theta_value = sine_value * alpha_norm
            rho_bar = -cosine * alpha_norm
            search_dir = right_vec - theta_value / rho_value * search_dir
    solution = solve_upper(lower_factor, iterate)
    fitted = forward(grouped, patterns, solution)
    return (solution, fitted)
```

```python
import jax
import jax.numpy as jnp
from jax import lax
from jax.experimental import pallas as pl
from jax.experimental.pallas import tpu as pltpu
from jax.sharding import PartitionSpec as P

NC = 1024
BLK = 64
KB = 4
B = 128
NB = NC // B
WIDTH = KB * BLK
TOL = 2e-6
CHECK = 2e-5
LIMIT = 300
ROUNDS = 4
DOUBLINGS = 5
STEPS = 9
CONTRACT_LANES = (((1,), (1,)), ((), ()))
MESH = pl.DeviceIdType.MESH

NEAR = [(i, d) for i in range(NB // 2) for d in range(NB // 2)]
PAIRS = [(4 * c + i, (4 * c + i + d) % NB) for c in range(2) for i, d in NEAR]
PAIRS = PAIRS[:16] + [(0, 4), (1, 5)] + PAIRS[16:] + [(6, 2), (7, 3)]
PER_CORE = len(PAIRS) // 2
INDEX = {pair: n for n, pair in enumerate(PAIRS)}

NZ, NY, NX = 8, 8, 4
HALF = PER_CORE * B
PART_A, PART_B, PART_C = 0, 512, 1024
SLAB = 512 // NZ
CELL = SLAB // NY
WIDE = (HALF - PART_C) // NX
SIDE = 192
THIN1 = SIDE // NY
THIN2 = (WIDE - SIDE) // NZ


def split2(x):
    hi = x.astype(jnp.bfloat16)
    return hi, (x - hi.astype(jnp.float32)).astype(jnp.bfloat16)


def split3(x):
    hi = x.astype(jnp.bfloat16)
    mid, lo = split2(x - hi.astype(jnp.float32))
    return hi, mid, lo


def dot_nt(x, y):
    return lax.dot_general(x, y, CONTRACT_LANES, preferred_element_type=jnp.float32)


def stacked(row):
    parts = [part.astype(jnp.float32) for part in split3(row)]
    line = lax.broadcasted_iota(jnp.int32, (16, row.shape[1]), 0)
    value = jnp.where(line == 0, parts[0], 0.0)
    value = jnp.where(line == 1, parts[1], value)
    return jnp.where(line == 2, parts[2], value).astype(jnp.bfloat16)


def pack(rows):
    line = lax.broadcasted_iota(jnp.int32, (NB, B), 0)
    value = jnp.where(line == 0, rows[0], 0.0)
    for j in range(1, NB):
        value = jnp.where(line == j, rows[j], value)
    return value


def dense_block(values, columns, dense_t, lanes):
    rows = lax.broadcasted_iota(jnp.int32, (NC, WIDTH), 0).astype(jnp.float32)
    first = lax.broadcasted_iota(jnp.int32, (NC, B), 1) < BLK
    for half in range(2):
        pair = values[half].astype(jnp.bfloat16)
        picks = [
            jnp.where(rows == columns[n : n + 1, :], 1.0, 0.0).astype(jnp.bfloat16)
            for n in (2 * half, 2 * half + 1)
        ]
        both = jnp.where(first, dot_nt(picks[0], pair), dot_nt(picks[1], pair))
        start = lanes + half * B
        dense_t[:NC, start : start + B] = both.astype(jnp.bfloat16)


def remote(src, dst, send, recv, device):
    moved = pltpu.make_async_remote_copy(
        src_ref=src, dst_ref=dst, send_sem=send, recv_sem=recv, device_id=device, device_id_type=MESH
    )
    moved.start()
    return moved


def greet(peers):
    barrier = pltpu.get_barrier_semaphore()
    for peer in peers:
        pl.semaphore_signal(barrier, inc=1, device_id=peer, device_id_type=MESH)
    return barrier


def position():
    place = lax.axis_index("rows")
    return place, lax.axis_index("grp"), place % 2, (place // 2) % NY, place // (2 * NY)


def reduce_kernel(
    ridge, values_in, pattern_in, targets_in, weights_in, operator, own_dense, mat, inverse, side, begin,
    values, pattern, targets, weights, raw, extra, there, extra_there, dense_t, gathered_m, columns, load_sem,
    send_raw, recv_raw, *rest,
):
    place, x, core, y, z = position()
    loads = [
        pltpu.make_async_copy(source, target, load_sem.at[n])
        for n, (source, target) in enumerate(
            ((values_in, values), (pattern_in, pattern), (targets_in, targets), (weights_in, weights))
        )
    ]
    for item in loads:
        item.start()

    def along_z(d):
        return (((z + d) % NZ) * 2 * NY + y * 2 + core, x)

    def along_y(d):
        return (z * 2 * NY + ((y + d) % NY) * 2 + core, x)

    def along_x(d):
        return (place, (x + d) % NX)

    sibling = (place + 1 - 2 * core, x)
    peers = [sibling]
    peers += [along_z(d) for d in range(1, NZ)] + [along_y(d) for d in range(1, NY)]
    peers += [along_x(d) for d in range(1, NX)]
    barrier = greet(peers)
    for item in loads:
        item.wait()
    raw[...] = values[...].astype(jnp.float32)
    lane = lax.broadcasted_iota(jnp.int32, (1, WIDTH), 1)
    for n in range(4):
        block = jnp.where(lane < BLK, pattern[n : n + 1, 0:1], pattern[n : n + 1, 1:2])
        after = jnp.where(lane < 3 * BLK, pattern[n : n + 1, 2:3], pattern[n : n + 1, 3:4])
        block = jnp.where(lane < 2 * BLK, block, after)
        extra[n : n + 1, :] = (block * BLK + lane % BLK).astype(jnp.float32)
    square = weights[...] * weights[...]
    extra[4:5, :] = square
    extra[5:6, :] = square * targets[...]
    extra[6:8, :] = jnp.zeros((2, WIDTH), jnp.float32)
    pl.semaphore_wait(barrier, len(peers))

    first = remote(raw, there, send_raw.at[0], recv_raw.at[0], sibling)
    second = remote(extra, extra_there, send_raw.at[1], recv_raw.at[1], sibling)
    dense_block(values, extra, dense_t, 0)
    own_dense[...] = dense_t[:NC, :WIDTH]
    first.wait()
    second.wait()
    dense_block(there, extra_there, dense_t, WIDTH)

    dense_t[NC:, :] = dense_t[: NC // 2, :]
    own = 4 * core

    def make_blocks(local, product):
        for i in range(NB // 2):
            start = pl.multiple_of((own + i) * B, B)
            block = product(start, start, 4 * B)
            for d in range(4):
                row = (4 * i + d) * B
                local[row : row + B, :] = block[:, d * B : (d + 1) * B]
        for i in range(2):
            start = pl.multiple_of((6 * core + i) * B, B)
            row = (16 + i) * B
            local[row : row + B, :] = product(start, pl.multiple_of(start + 4 * B, B), B)

    def plain(first, second, count):
        return dot_nt(dense_t[pl.ds(first, B), :], dense_t[pl.ds(second, count), :])

    square = jnp.concatenate([extra[4:5, :], extra_there[4:5, :]], axis=1)

    def weighted(first, second, count):
        hi, lo = split2(dense_t[pl.ds(first, B), :].astype(jnp.float32) * square)
        others = dense_t[pl.ds(second, count), :]
        return dot_nt(hi, others) + dot_nt(lo, others)

    def rows(start, count):
        return pl.ds(pl.multiple_of(start, 8), count)

    def total(mine, arrived):
        value = mine
        for n in range(arrived.shape[0]):
            value = value + arrived[n]
        return value

    def ordered(slots):
        value = slots[0]
        for n in range(1, slots.shape[0]):
            value = value + slots[n]
        return value

    sent = []

    def scatter(axis, source, start, count, landing, send, recv, base):
        step, me, size = axis
        out = []
        for d in range(1, size):
            target = (me + d) % size
            piece = source.at[rows(start + target * count, count)]
            out.append(remote(piece, landing.at[d - 1], send.at[base + d - 1], recv.at[base + d - 1], step(d)))
        sent.extend(out)
        return out

    def spread(axis, source, landing, send, recv, base):
        step, _, size = axis
        out = []
        for d in range(1, size):
            out.append(remote(source, landing, send.at[base + d - 1], recv.at[base + d - 1], step(d)))
        sent.extend(out)
        return out

    def arrive(copies):
        for item in copies:
            item.wait_recv()

    axis_z, axis_y, axis_x = (along_z, z, NZ), (along_y, y, NY), (along_x, x, NX)
    half = core * HALF

    def job(refs, result):
        local, in_a, in_b, in_c, slab_a, slab_b, wide_c, in_a2, in_b2, in_c1, in_c2, in_cells, in_thin1, in_thin2 = refs[:14]
        send1, recv1, send2, recv2, send3, recv3, send4, recv4, send5, recv5, send6, recv6 = refs[14:]

        def place_of(start, count):
            return result.at[rows(half + start, count)]

        c1 = scatter(axis_x, local, PART_C, WIDE, in_c, send1, recv1, 0)
        a1 = scatter(axis_z, local, PART_A, SLAB, in_a, send1, recv1, 3)
        b1 = scatter(axis_y, local, PART_B, SLAB, in_b, send1, recv1, 10)
        yield
        arrive(a1)
        slab_a[...] = total(local[rows(PART_A + z * SLAB, SLAB), :], in_a)
        a2 = scatter(axis_y, slab_a, 0, CELL, in_a2, send2, recv2, 0)
        arrive(b1)
        slab_b[...] = total(local[rows(PART_B + y * SLAB, SLAB), :], in_b)
        b2 = scatter(axis_z, slab_b, 0, CELL, in_b2, send2, recv2, 7)
        arrive(c1)
        wide_c[...] = total(local[rows(PART_C + x * WIDE, WIDE), :], in_c)
        d2 = scatter(axis_y, wide_c, 0, THIN1, in_c1, send2, recv2, 14)
        e2 = scatter(axis_z, wide_c, SIDE, THIN2, in_c2, send2, recv2, 21)
        yield
        arrive(a2)
        in_cells[x, :CELL, :] = total(slab_a[rows(y * CELL, CELL), :], in_a2)
        arrive(b2)
        in_cells[x, CELL:, :] = total(slab_b[rows(z * CELL, CELL), :], in_b2)
        ab3 = spread(axis_x, in_cells.at[x], in_cells.at[x], send3, recv3, 0)
        arrive(d2)
        in_thin1[z] = total(wide_c[rows(y * THIN1, THIN1), :], in_c1)
        d3 = spread(axis_z, in_thin1.at[z], in_thin1.at[z], send3, recv3, 3)
        arrive(e2)
        in_thin2[y] = total(wide_c[rows(SIDE + z * THIN2, THIN2), :], in_c2)
        e3 = spread(axis_y, in_thin2.at[y], in_thin2.at[y], send3, recv3, 10)
        yield
        cell_a = place_of(PART_A + z * SLAB + y * CELL, CELL)
        cell_b = place_of(PART_B + y * SLAB + z * CELL, CELL)
        thin_d = place_of(PART_C + x * WIDE + y * THIN1, THIN1)
        thin_e = place_of(PART_C + x * WIDE + SIDE + z * THIN2, THIN2)
        arrive(ab3)
        both = ordered(in_cells)
        cell_a[...] = both[:CELL]
        cell_b[...] = both[CELL:]
        a4 = spread(axis_y, cell_a, cell_a, send4, recv4, 0)
        b4 = spread(axis_z, cell_b, cell_b, send4, recv4, 7)
        arrive(d3)
        thin_d[...] = ordered(in_thin1)
        d4 = spread(axis_y, thin_d, thin_d, send4, recv4, 14)
        arrive(e3)
        thin_e[...] = ordered(in_thin2)
        e4 = spread(axis_z, thin_e, thin_e, send4, recv4, 21)
        yield
        big_a, big_b = place_of(PART_A + z * SLAB, SLAB), place_of(PART_B + y * SLAB, SLAB)
        big_c = place_of(PART_C + x * WIDE, WIDE)
        arrive(d4)
        arrive(e4)
        c5 = spread(axis_x, big_c, big_c, send5, recv5, 0)
        arrive(a4)
        a5 = spread(axis_z, big_a, big_a, send5, recv5, 3)
        arrive(b4)
        b5 = spread(axis_y, big_b, big_b, send5, recv5, 10)
        yield

        def across(start, count, n):
            block = place_of(start, count)
            item = remote(block, block, send6.at[n], recv6.at[n], sibling)
            sent.append(item)
            return item

        arrive(a5)
        last = [across(PART_A, PART_B - PART_A, 0)]
        arrive(b5)
        last.append(across(PART_B, PART_C - PART_B, 1))
        arrive(c5)
        last.append(across(PART_C, HALF - PART_C, 2))
        yield
        arrive(last)
        yield

    count = len(rest) // 2
    locals_m, locals_w = rest[:count], rest[count:]
    make_blocks(locals_m[0], plain)
    aims = stacked(jnp.concatenate([extra[5:6, :], extra_there[5:6, :]], axis=1))
    for c in range(NC // BLK):
        line = dot_nt(aims, dense_t[c * BLK : (c + 1) * BLK, :])
        locals_m[0][BLK + c : BLK + c + 1, :BLK] = jnp.sum(line, axis=0, keepdims=True)
    job_m = job(locals_m, gathered_m)
    next(job_m)
    make_blocks(locals_w[0], weighted)
    job_w = job(locals_w, operator)
    next(job_w)
    for _ in range(4):
        next(job_m)
        next(job_w)
    next(job_m)
    next(job_m)

    unpack(ridge, gathered_m, mat, side)
    invert_blocks(mat, inverse)
    next(job_w)
    begin[...] = first_steps(mat, inverse, columns, side[...])
    next(job_w)
    for item in sent:
        item.wait_send()


def diagonal():
    shape = (B, B)
    return lax.broadcasted_iota(jnp.int32, shape, 0) == lax.broadcasted_iota(jnp.int32, shape, 1)


def to_row(column):
    return jnp.sum(jnp.where(diagonal(), column, 0.0), axis=0, keepdims=True)


def to_column(row):
    return jnp.sum(jnp.where(diagonal(), row, 0.0), axis=1, keepdims=True)


def dot(x, y):
    return jnp.sum(jnp.sum(x * y, axis=0, keepdims=True), axis=1, keepdims=True)


def block_rows(block, column):
    return jnp.sum((block * column).reshape(B // 8, 8, B), axis=0)


def spread_columns(vector, columns):
    for j in range(NB):
        columns[j] = jnp.broadcast_to(to_column(vector[j : j + 1, :]), (B, B))


def apply_full(mat, columns):
    acc = [None] * NB
    for i in range(NB):
        column = columns[i]
        for j in range(NB):
            part = block_rows(mat[i, j], column)
            acc[j] = part if acc[j] is None else acc[j] + part
    return pack([jnp.sum(part, axis=0, keepdims=True) for part in acc])


def apply_diag(inverse, vector, columns):
    rows = []
    for b in range(NB):
        column = jnp.sum(inverse[b] * vector[b : b + 1, :], axis=1, keepdims=True)
        column = jnp.broadcast_to(column, (B, B))
        columns[b] = column
        rows.append(to_row(column))
    return pack(rows)


def invert_blocks(mat, inverse):
    identity = diagonal()
    one = jnp.where(identity, 1.0, 0.0)
    upper = lax.broadcasted_iota(jnp.int32, (B, B), 0) < BLK
    left = lax.broadcasted_iota(jnp.int32, (B, B), 1) < BLK
    errors, scales = [], []
    for b in range(NB):
        block = jnp.where(upper == left, mat[b, b], 0.0)
        middle = jnp.where(identity, block, 0.0)
        row = lax.rsqrt(jnp.sum(middle, axis=0, keepdims=True))
        column = lax.rsqrt(jnp.sum(middle, axis=1, keepdims=True))
        block = block * row * column
        bound = jnp.max(jnp.sum(jnp.abs(block), axis=1, keepdims=True), axis=0, keepdims=True)
        errors.append(one - block / bound)
        scales.append(row * column / bound)

    def times(rows, square):
        (top, rest), (hi, lo) = split2(rows), split2(square)
        both = jnp.dot(top, hi, preferred_element_type=jnp.float32)
        both = both + jnp.dot(rest, hi, preferred_element_type=jnp.float32)
        return both + jnp.dot(top, lo, preferred_element_type=jnp.float32)

    sums = [one + error for error in errors]
    errors = [times(error, error) for error in errors]
    for n in range(DOUBLINGS):
        for b in range(NB):
            if n + 1 == DOUBLINGS:
                sums[b] = sums[b] + times(sums[b], errors[b])
            else:
                both = times(jnp.concatenate([errors[b], sums[b]], axis=0), errors[b])
                errors[b] = both[:B]
                sums[b] = sums[b] + both[B:]
    for b in range(NB):
        inverse[b] = sums[b] * scales[b]


def eliminate(mat, spare, right, columns, out):
    spare[...] = mat[...]
    spread_columns(right, columns)
    lane = lax.broadcasted_iota(jnp.int32, (B, B), 1)
    line = lax.broadcasted_iota(jnp.int32, (B, B), 0)

    def pivot(k, carry):
        kb, kr = k // B, k % B
        rows = [spare[kb, j, pl.ds(kr, 1), :] for j in range(NB)]
        entry = columns[kb, pl.ds(kr, 1), :]
        value = jnp.sum(jnp.where(lane[:1] == kr, spare[kb, kb, pl.ds(kr, 1), :], 0.0), axis=1, keepdims=True)

        def sweep(i, carry):
            factor = jnp.sum(jnp.where(lane == kr, spare[i, kb], 0.0), axis=1, keepdims=True) / value
            factor = jnp.where((line == kr) & (i == kb), 0.0, factor)
            for j in range(NB):
                spare[i, j] = spare[i, j] - factor * rows[j]
            columns[i] = columns[i] - factor * entry
            return carry

        return lax.fori_loop(0, NB, sweep, carry)

    lax.fori_loop(0, NC, pivot, 0)
    rows = []
    for b in range(NB):
        scale = jnp.sum(jnp.where(diagonal(), spare[b, b], 0.0), axis=1, keepdims=True)
        rows.append(to_row(columns[b] / scale))
    out[...] = pack(rows)


def first_steps(mat, inverse, columns, right):
    zero = jnp.zeros((NB, B), jnp.float32)
    pre = apply_diag(inverse, right, columns)
    size = dot(right, pre)
    bound = (TOL * TOL) * size
    image = apply_full(mat, columns)

    def advance(_, carry):
        res, pre, image, step, moved, total, size, ratio, length = carry
        step = pre + ratio * step
        moved = image + ratio * moved
        total = total + length * step
        res = res - length * moved
        pre = apply_diag(inverse, res, columns)
        latest = dot(res, pre)
        image = apply_full(mat, columns)
        active = latest > bound
        ratio = jnp.where(active, latest / size, 0.0)
        further = jnp.where(active, latest / (dot(image, pre) - ratio * latest / length), 0.0)
        return res, pre, image, step, moved, total, latest, ratio, further

    start = (right, pre, image, zero, zero, zero, size, jnp.zeros((1, 1), jnp.float32), size / dot(image, pre))
    carry = lax.fori_loop(0, STEPS - 1, advance, start)
    res, pre, image, step, moved, total, size, ratio, length = carry
    return total + length * (pre + ratio * step)


def solve(mat, inverse, spare, columns, right, out, begin=None):
    zero = jnp.zeros((NB, B), jnp.float32)

    def inner(res, pre, size, bound):
        image = apply_full(mat, columns)

        def going(carry):
            return (carry[0] < LIMIT) & (carry[1] > bound)

        def advance(carry):
            count, _, res, pre, image, step, moved, total, size, ratio, length = carry
            step = pre + ratio * step
            moved = image + ratio * moved
            total = total + length * step
            res = res - length * moved
            pre = apply_diag(inverse, res, columns)
            latest = dot(res, pre)
            image = apply_full(mat, columns)
            ratio = latest / size
            length = latest / (dot(image, pre) - ratio * latest / length)
            return count + 1, latest[0, 0], res, pre, image, step, moved, total, latest, ratio, length

        start = (
            jnp.int32(0), size[0, 0], res, pre, image, zero, zero, zero,
            size, jnp.zeros((1, 1), jnp.float32), size / dot(image, pre),
        )
        return lax.while_loop(going, advance, start)[7]

    def residual(value):
        spread_columns(value, columns)
        res = right - apply_full(mat, columns)
        pre = apply_diag(inverse, res, columns)
        return res, pre, dot(res, pre)

    pre = apply_diag(inverse, right, columns)
    size = dot(right, pre)
    first = size[0, 0]
    if begin is None:
        out[...] = zero
        begun = (jnp.int32(0), first, right, pre, size)
    else:
        out[...] = begin
        res, pre, size = residual(begin)
        begun = (jnp.int32(0), size[0, 0], res, pre, size)

    def unsolved(carry):
        return (carry[0] < ROUNDS) & (carry[1] > CHECK * CHECK * first)

    def improve(carry):
        count, _, res, pre, size = carry
        out[...] += inner(res, pre, size, TOL * TOL * first)
        res, pre, size = residual(out[...])
        return count + 1, size[0, 0], res, pre, size

    final = lax.while_loop(unsolved, improve, begun)[1]

    @pl.when(jnp.logical_not(final <= CHECK * CHECK * first))
    def _():
        eliminate(mat, spare, right, columns, out)


def corner_fixed(block):
    low = lax.broadcasted_iota(jnp.int32, (B, B), 0) >= BLK
    low = low & (lax.broadcasted_iota(jnp.int32, (B, B), 1) < BLK)
    return jnp.where(low, block.T, block)


def unpack(ridge, grams, mat, side):
    identity = diagonal()
    left = lax.broadcasted_iota(jnp.int32, (1, B), 1) < BLK
    sides = []
    for j in range(NB):
        even = grams[BLK + 2 * j : BLK + 2 * j + 1, :]
        odd = grams[BLK + 2 * j + 1 : BLK + 2 * j + 2, :]
        sides.append(jnp.where(left, even, pltpu.roll(odd, BLK, 1)))
    side[...] = pack(sides)
    for n, (i, j) in enumerate(PAIRS):
        block = grams[n * B : (n + 1) * B, :]
        if n % PER_CORE == 0:
            block = corner_fixed(block)
        if i == j:
            mat[i, i] = block + jnp.where(identity, ridge, 0.0)
        else:
            mat[i, j] = block
            mat[j, i] = block.T


def apply_operator(blocks, ridge, vector, columns):
    spread_columns(vector, columns)
    down = [jnp.zeros((8, B), jnp.float32)] * NB
    rows = []
    for i in range(NB):
        column = columns[i]
        across = jnp.zeros((B, B), jnp.float32)
        for j in range(NB):
            if (i, j) in INDEX:
                block = blocks[INDEX[i, j]]
                down[j] = down[j] + block_rows(block, column)
                if j != i:
                    across = across + block * vector[j : j + 1, :]
        rows.append(to_row(jnp.sum(across, axis=1, keepdims=True)))
    total = [jnp.sum(part, axis=0, keepdims=True) + row for part, row in zip(down, rows)]
    return pack(total) + ridge * vector


def solver_kernel(ridge, blocks, dense_t, mat, inverse, side, begin, solution, fitted, spare, columns, first, second):
    g = side[...]
    solve(mat, inverse, spare, columns, g, first, begin[...])
    z = first[...]
    h = apply_operator(blocks, ridge, z, columns)
    gain = dot(g, z)
    length = gain / dot(z, h)
    rest = g - length * h
    solve(mat, inverse, spare, columns, rest, second)
    s = second[...]
    latest = dot(rest, s)
    ratio = latest / gain
    image = apply_operator(blocks, ridge, s, columns) + ratio * h
    step = s + ratio * z
    curve = dot(step, image)
    x = length * z + jnp.where(curve > 0.0, latest / curve, 0.0) * step
    solution[...] = x

    spread_columns(x, columns)
    for half in range(2):
        acc = jnp.zeros((8, B), jnp.float32)
        for j in range(NB):
            part = dense_t[j * B : (j + 1) * B, half * B : (half + 1) * B].astype(jnp.float32)
            acc = acc + block_rows(part, columns[j])
        fitted[half : half + 1, :] = jnp.sum(acc, axis=0, keepdims=True)


def space(*shape):
    return pltpu.VMEM(shape, jnp.float32)


def shaped(*shape):
    return jax.ShapeDtypeStruct(shape, jnp.float32)


WHOLE = pl.BlockSpec(memory_space=pltpu.VMEM)
LIMITS = dict(vmem_limit_bytes=32 << 20)


def body(values, pattern, targets, root_weights):
    tiles = values.shape[0]
    own_rows = tiles * BLK
    rows_total = own_rows * lax.axis_size("rows") * lax.axis_size("grp")
    ridge = rows_total / (2.0 * NC)
    job_space = [
        space(HALF, B),
        space(NZ - 1, SLAB, B),
        space(NY - 1, SLAB, B),
        space(NX - 1, WIDE, B),
        space(SLAB, B),
        space(SLAB, B),
        space(WIDE, B),
        space(NY - 1, CELL, B),
        space(NZ - 1, CELL, B),
        space(NY - 1, THIN1, B),
        space(NZ - 1, THIN2, B),
        space(NX, 2 * CELL, B),
        space(NZ, THIN1, B),
        space(NY, THIN2, B),
    ] + [pltpu.SemaphoreType.DMA((n,)) for n in (17, 17, 28, 28, 17, 17, 28, 28, 17, 17, 3, 3)]
    operator, dense_t, mat, inverse, side, begin = pl.pallas_call(
        lambda *refs: reduce_kernel(ridge, *refs),
        out_shape=(
            shaped(2 * HALF, B),
            jax.ShapeDtypeStruct((NC, own_rows), jnp.bfloat16),
            shaped(NB, NB, B, B),
            shaped(NB, B, B),
            shaped(NB, B),
            shaped(NB, B),
        ),
        in_specs=[pl.BlockSpec(memory_space=pltpu.HBM)] * 4,
        out_specs=(WHOLE,) * 6,
        scratch_shapes=[
            pltpu.VMEM((2, B, WIDTH), jnp.bfloat16),
            pltpu.VMEM(pattern.shape, jnp.int32),
            space(1, WIDTH),
            space(1, WIDTH),
            space(2, B, WIDTH),
            space(8, WIDTH),
            space(2, B, WIDTH),
            space(8, WIDTH),
            pltpu.VMEM((NC + NC // 2, 2 * WIDTH), jnp.bfloat16),
            space(2 * HALF, B),
            space(NB, B, B),
            pltpu.SemaphoreType.DMA((4,)),
            pltpu.SemaphoreType.DMA((2,)),
            pltpu.SemaphoreType.DMA((2,)),
        ]
        + job_space * 2,
        compiler_params=pltpu.CompilerParams(collective_id=0, has_side_effects=True, **LIMITS),
    )(
        *(
            pltpu.with_memory_space_constraint(operand, pltpu.HBM)
            for operand in (
                values.reshape(tiles // 2, 2 * BLK, WIDTH), pattern, targets.reshape(1, -1), root_weights.reshape(1, -1)
            )
        )
    )
    solution_rows, fitted = pl.pallas_call(
        lambda *refs: solver_kernel(ridge, *refs),
        out_shape=(shaped(NB, B), shaped(own_rows // B, B)),
        in_specs=[WHOLE] * 6,
        out_specs=(WHOLE,) * 2,
        scratch_shapes=[space(NB, NB, B, B), space(NB, B, B), space(NB, B), space(NB, B)],
        compiler_params=pltpu.CompilerParams(**LIMITS),
    )(operator.reshape(len(PAIRS), B, B), dense_t, mat, inverse, side, begin)
    return solution_rows.reshape(-1), fitted.reshape(-1)


def solution(mesh):
    in_specs = (
        P(("rows", "grp"), None, None),
        P(("rows", "grp"), None),
        P(("rows", "grp")),
        P(("rows", "grp")),
    )
    out_specs = (P(), P(("rows", "grp")))
    return jax.shard_map(body, mesh=mesh, in_specs=in_specs, out_specs=out_specs, check_vma=False)
```

```python
import jax
import jax.numpy as jnp
from jax import lax
from jax.experimental import pallas as pl
from jax.experimental.pallas import tpu as pltpu
from jax.sharding import PartitionSpec as P

NC = 1024
BLK = 64
KB = 4
B = 128
NB = NC // B
WIDTH = KB * BLK
TOL = 2e-6
CHECK = 2e-5
LIMIT = 300
ROUNDS = 4
DOUBLINGS = 5
STEPS = 9
CONTRACT_LANES = (((1,), (1,)), ((), ()))
MESH = pl.DeviceIdType.MESH

NEAR = [(i, d) for i in range(NB // 2) for d in range(NB // 2)]
PAIRS = [(4 * c + i, (4 * c + i + d) % NB) for c in range(2) for i, d in NEAR]
PAIRS = PAIRS[:16] + [(0, 4), (1, 5)] + PAIRS[16:] + [(6, 2), (7, 3)]
PER_CORE = len(PAIRS) // 2
INDEX = {pair: n for n, pair in enumerate(PAIRS)}

NZ, NY, NX = 8, 8, 4
HALF = PER_CORE * B
PART_A, PART_B, PART_C = 0, 512, 1024
SLAB = 512 // NZ
CELL = SLAB // NY
WIDE = (HALF - PART_C) // NX
SIDE = 192
THIN1 = SIDE // NY
THIN2 = (WIDE - SIDE) // NZ


def split2(x):
    hi = x.astype(jnp.bfloat16)
    return hi, (x - hi.astype(jnp.float32)).astype(jnp.bfloat16)


def split3(x):
    hi = x.astype(jnp.bfloat16)
    mid, lo = split2(x - hi.astype(jnp.float32))
    return hi, mid, lo


def dot_nt(x, y):
    return lax.dot_general(x, y, CONTRACT_LANES, preferred_element_type=jnp.float32)


def stacked(row):
    parts = [part.astype(jnp.float32) for part in split3(row)]
    line = lax.broadcasted_iota(jnp.int32, (16, row.shape[1]), 0)
    value = jnp.where(line == 0, parts[0], 0.0)
    value = jnp.where(line == 1, parts[1], value)
    return jnp.where(line == 2, parts[2], value).astype(jnp.bfloat16)


def pack(rows):
    line = lax.broadcasted_iota(jnp.int32, (NB, B), 0)
    value = jnp.where(line == 0, rows[0], 0.0)
    for j in range(1, NB):
        value = jnp.where(line == j, rows[j], value)
    return value


def dense_block(values, columns, dense_t, lanes):
    rows = lax.broadcasted_iota(jnp.int32, (NC, WIDTH), 0).astype(jnp.float32)
    first = lax.broadcasted_iota(jnp.int32, (NC, B), 1) < BLK
    for half in range(2):
        pair = values[half].astype(jnp.bfloat16)
        picks = [
            jnp.where(rows == columns[n : n + 1, :], 1.0, 0.0).astype(jnp.bfloat16)
            for n in (2 * half, 2 * half + 1)
        ]
        both = jnp.where(first, dot_nt(picks[0], pair), dot_nt(picks[1], pair))
        start = lanes + half * B
        dense_t[:NC, start : start + B] = both.astype(jnp.bfloat16)


def remote(src, dst, send, recv, device):
    moved = pltpu.make_async_remote_copy(
        src_ref=src, dst_ref=dst, send_sem=send, recv_sem=recv, device_id=device, device_id_type=MESH
    )
    moved.start()
    return moved


def greet(peers):
    barrier = pltpu.get_barrier_semaphore()
    for peer in peers:
        pl.semaphore_signal(barrier, inc=1, device_id=peer, device_id_type=MESH)
    return barrier


def position():
    place = lax.axis_index("rows")
    return place, lax.axis_index("grp"), place % 2, (place // 2) % NY, place // (2 * NY)


def reduce_kernel(
    ridge, values_in, pattern_in, targets_in, weights_in, operator, own_dense, mat, inverse, side, begin, left,
    values, pattern, targets, weights, raw, extra, there, extra_there, dense_t, gathered_m, columns, load_sem,
    send_raw, recv_raw, *rest,
):
    place, x, core, y, z = position()
    loads = [
        pltpu.make_async_copy(source, target, load_sem.at[n])
        for n, (source, target) in enumerate(
            ((values_in, values), (pattern_in, pattern), (targets_in, targets), (weights_in, weights))
        )
    ]
    for item in loads:
        item.start()

    def along_z(d):
        return (((z + d) % NZ) * 2 * NY + y * 2 + core, x)

    def along_y(d):
        return (z * 2 * NY + ((y + d) % NY) * 2 + core, x)

    def along_x(d):
        return (place, (x + d) % NX)

    sibling = (place + 1 - 2 * core, x)
    peers = [sibling]
    peers += [along_z(d) for d in range(1, NZ)] + [along_y(d) for d in range(1, NY)]
    peers += [along_x(d) for d in range(1, NX)]
    barrier = greet(peers)
    for item in loads:
        item.wait()
    raw[...] = values[...].astype(jnp.float32)
    lane = lax.broadcasted_iota(jnp.int32, (1, WIDTH), 1)
    for n in range(4):
        block = jnp.where(lane < BLK, pattern[n : n + 1, 0:1], pattern[n : n + 1, 1:2])
        after = jnp.where(lane < 3 * BLK, pattern[n : n + 1, 2:3], pattern[n : n + 1, 3:4])
        block = jnp.where(lane < 2 * BLK, block, after)
        extra[n : n + 1, :] = (block * BLK + lane % BLK).astype(jnp.float32)
    square = weights[...] * weights[...]
    extra[4:5, :] = square
    extra[5:6, :] = square * targets[...]
    extra[6:8, :] = jnp.zeros((2, WIDTH), jnp.float32)
    pl.semaphore_wait(barrier, len(peers))

    first = remote(raw, there, send_raw.at[0], recv_raw.at[0], sibling)
    second = remote(extra, extra_there, send_raw.at[1], recv_raw.at[1], sibling)
    dense_block(values, extra, dense_t, 0)
    own_dense[...] = dense_t[:NC, :WIDTH]
    first.wait()
    second.wait()
    dense_block(there, extra_there, dense_t, WIDTH)

    dense_t[NC:, :] = dense_t[: NC // 2, :]
    own = 4 * core

    def near_blocks(local, product, which):
        for i in which:
            start = pl.multiple_of((own + i) * B, B)
            block = product(start, start, 4 * B)
            for d in range(4):
                row = (4 * i + d) * B
                local[row : row + B, :] = block[:, d * B : (d + 1) * B]

    def far_blocks(local, product):
        for i in range(2):
            start = pl.multiple_of((6 * core + i) * B, B)
            row = (16 + i) * B
            local[row : row + B, :] = product(start, pl.multiple_of(start + 4 * B, B), B)

    def plain(first, second, count):
        return dot_nt(dense_t[pl.ds(first, B), :], dense_t[pl.ds(second, count), :])

    square = jnp.concatenate([extra[4:5, :], extra_there[4:5, :]], axis=1)

    def weighted(first, second, count):
        hi, lo = split2(dense_t[pl.ds(first, B), :].astype(jnp.float32) * square)
        others = dense_t[pl.ds(second, count), :]
        return dot_nt(hi, others) + dot_nt(lo, others)

    def rows(start, count):
        return pl.ds(pl.multiple_of(start, 8), count)

    def total(mine, arrived):
        value = mine
        for n in range(arrived.shape[0]):
            value = value + arrived[n]
        return value

    def ordered(slots):
        value = slots[0]
        for n in range(1, slots.shape[0]):
            value = value + slots[n]
        return value

    def settle(ref, sem):
        pltpu.make_async_copy(ref, ref, sem).wait()

    def scatter(axis, piece, landing, send, recv):
        step, me, size = axis
        for d in range(1, size):
            remote(piece((me + d) % size), landing.at[d - 1], send, recv, step(d))

    def spread(axis, block, send, recv):
        step, _, size = axis
        for d in range(1, size):
            remote(block, block, send, recv, step(d))

    axis_z, axis_y, axis_x = (along_z, z, NZ), (along_y, y, NY), (along_x, x, NX)
    half = core * HALF

    def job(refs, result, product, finish):
        local, in_a, in_b, in_c, mix_y, mix_z, in_y, in_z, in_cells, in_thin1, in_thin2, out_y, out_z, send, recv = refs
        sizes = []

        def sems(count):
            sizes.append(count)
            return send.at[len(sizes) - 1], recv.at[len(sizes) - 1]

        def place_of(start, count):
            return result.at[rows(half + start, count)]

        def part(start, count):
            return lambda k: local.at[rows(start + k * count, count)]

        near_blocks(local, product, (2, 3))
        far_blocks(local, product)
        sem_c = sems((NX - 1) * WIDE)
        scatter(axis_x, part(PART_C, WIDE), in_c, *sem_c)
        near_blocks(local, product, (1,))
        sem_b = sems((NY - 1) * SLAB)
        scatter(axis_y, part(PART_B, SLAB), in_b, *sem_b)
        near_blocks(local, product, (0,))
        finish(local)
        sem_a = sems((NZ - 1) * SLAB)
        scatter(axis_z, part(PART_A, SLAB), in_a, *sem_a)
        yield
        settle(in_a, sem_a[1])
        slab = total(local[rows(PART_A + z * SLAB, SLAB), :], in_a)
        for k in range(NY):
            mix_y[k, :CELL, :] = slab[k * CELL : (k + 1) * CELL]
        settle(in_b, sem_b[1])
        slab = total(local[rows(PART_B + y * SLAB, SLAB), :], in_b)
        for k in range(NZ):
            mix_z[k, :CELL, :] = slab[k * CELL : (k + 1) * CELL]
        settle(in_c, sem_c[1])
        slab = total(local[rows(PART_C + x * WIDE, WIDE), :], in_c)
        for k in range(NY):
            mix_y[k, CELL:, :] = slab[k * THIN1 : (k + 1) * THIN1]
        for k in range(NZ):
            mix_z[k, CELL:, :] = slab[SIDE + k * THIN2 : SIDE + (k + 1) * THIN2]
        sem_y, sem_z = sems((NY - 1) * (CELL + THIN1)), sems((NZ - 1) * (CELL + THIN2))
        scatter(axis_y, lambda k: mix_y.at[k], in_y, *sem_y)
        scatter(axis_z, lambda k: mix_z.at[k], in_z, *sem_z)
        yield
        settle(in_y, sem_y[1])
        mixed = total(mix_y[y], in_y)
        in_cells[x, :CELL, :] = mixed[:CELL]
        in_thin1[z] = mixed[CELL:]
        sem_1 = sems((NZ - 1) * THIN1)
        spread(axis_z, in_thin1.at[z], *sem_1)
        settle(in_z, sem_z[1])
        mixed = total(mix_z[z], in_z)
        in_cells[x, CELL:, :] = mixed[:CELL]
        in_thin2[y] = mixed[CELL:]
        sem_2, sem_3 = sems((NY - 1) * THIN2), sems((NX - 1) * 2 * CELL)
        spread(axis_y, in_thin2.at[y], *sem_2)
        spread(axis_x, in_cells.at[x], *sem_3)
        yield
        settle(in_cells.at[pl.ds(0, NX - 1)], sem_3[1])
        both = ordered(in_cells)
        settle(in_thin1.at[pl.ds(0, NZ - 1)], sem_1[1])
        out_y[y, :CELL, :] = both[:CELL]
        out_y[y, CELL:, :] = ordered(in_thin1)
        sem_y = sems((NY - 1) * (CELL + THIN1))
        spread(axis_y, out_y.at[y], *sem_y)
        settle(in_thin2.at[pl.ds(0, NY - 1)], sem_2[1])
        out_z[z, :CELL, :] = both[CELL:]
        out_z[z, CELL:, :] = ordered(in_thin2)
        sem_z = sems((NZ - 1) * (CELL + THIN2))
        spread(axis_z, out_z.at[z], *sem_z)
        yield
        big_a, big_b = place_of(PART_A + z * SLAB, SLAB), place_of(PART_B + y * SLAB, SLAB)
        big_c = place_of(PART_C + x * WIDE, WIDE)
        settle(out_y.at[pl.ds(0, NY - 1)], sem_y[1])
        settle(out_z.at[pl.ds(0, NZ - 1)], sem_z[1])
        big_c[:SIDE, :] = out_y[:, CELL:, :].reshape(SIDE, B)
        big_c[SIDE:, :] = out_z[:, CELL:, :].reshape(WIDE - SIDE, B)
        sem_c = sems((NX - 1) * WIDE)
        spread(axis_x, big_c, *sem_c)
        big_a[...] = out_y[:, :CELL, :].reshape(SLAB, B)
        sem_a = sems((NZ - 1) * SLAB)
        spread(axis_z, big_a, *sem_a)
        big_b[...] = out_z[:, :CELL, :].reshape(SLAB, B)
        sem_b = sems((NY - 1) * SLAB)
        spread(axis_y, big_b, *sem_b)
        yield
        across = []
        for start, count, (_, arrived) in (
            (PART_A, PART_B - PART_A, sem_a), (PART_B, PART_C - PART_B, sem_b), (PART_C, HALF - PART_C, sem_c)
        ):
            settle(local.at[pl.ds(0, sizes_of(start))], arrived)
            pair = sems(count)
            block = place_of(start, count)
            remote(block, block, *pair, sibling)
            across.append((block, pair[1]))
        yield
        for block, arrived in across:
            settle(block, arrived)
        yield
        for n, moved in enumerate(sizes):
            settle(local.at[pl.ds(0, moved)], send.at[n])
        yield

    def sizes_of(start):
        return {PART_A: (NZ - 1) * SLAB, PART_B: (NY - 1) * SLAB, PART_C: (NX - 1) * WIDE}[start]

    count = len(rest) // 2
    locals_m, locals_w = rest[:count], rest[count:]
    aims = stacked(jnp.concatenate([extra[5:6, :], extra_there[5:6, :]], axis=1))

    def add_side(local):
        for c in range(NC // BLK):
            line = dot_nt(aims, dense_t[c * BLK : (c + 1) * BLK, :])
            local[BLK + c : BLK + c + 1, :BLK] = jnp.sum(line, axis=0, keepdims=True)

    job_m = job(locals_m, gathered_m, plain, add_side)
    job_w = job(locals_w, operator, weighted, lambda local: None)
    next(job_m)
    next(job_w)
    for _ in range(4):
        next(job_m)
        next(job_w)
    next(job_m)
    unpack(ridge, gathered_m, mat, core)
    next(job_m)
    unpack(ridge, gathered_m, mat, 1 - core)
    side[...] = right_side(gathered_m)

    invert_blocks(mat, inverse)
    advance, finish, state = first_steps(mat, inverse, columns, side[...])
    state = lax.fori_loop(0, STEPS // 2, advance, state)
    next(job_w)
    state = lax.fori_loop(STEPS // 2, STEPS - 1, advance, state)
    value = finish(state)
    begin[...] = value
    spread_columns(value, columns)
    left[...] = side[...] - apply_full(mat, columns)
    next(job_w)
    next(job_m)
    next(job_w)


def diagonal():
    shape = (B, B)
    return lax.broadcasted_iota(jnp.int32, shape, 0) == lax.broadcasted_iota(jnp.int32, shape, 1)


def to_row(column):
    return jnp.sum(jnp.where(diagonal(), column, 0.0), axis=0, keepdims=True)


def to_column(row):
    return jnp.sum(jnp.where(diagonal(), row, 0.0), axis=1, keepdims=True)


def dot(x, y):
    return jnp.sum(jnp.sum(x * y, axis=0, keepdims=True), axis=1, keepdims=True)


def block_rows(block, column):
    return jnp.sum((block * column).reshape(B // 8, 8, B), axis=0)


def spread_columns(vector, columns):
    for j in range(NB):
        columns[j] = jnp.broadcast_to(to_column(vector[j : j + 1, :]), (B, B))


def apply_full(mat, columns):
    acc = [None] * NB
    for i in range(NB):
        column = columns[i]
        for j in range(NB):
            part = block_rows(mat[i, j], column)
            acc[j] = part if acc[j] is None else acc[j] + part
    return pack([jnp.sum(part, axis=0, keepdims=True) for part in acc])


def apply_diag(inverse, vector, columns):
    rows = []
    for b in range(NB):
        column = jnp.sum(inverse[b] * vector[b : b + 1, :], axis=1, keepdims=True)
        column = jnp.broadcast_to(column, (B, B))
        columns[b] = column
        rows.append(to_row(column))
    return pack(rows)


def invert_blocks(mat, inverse):
    identity = diagonal()
    one = jnp.where(identity, 1.0, 0.0)
    upper = lax.broadcasted_iota(jnp.int32, (B, B), 0) < BLK
    left = lax.broadcasted_iota(jnp.int32, (B, B), 1) < BLK
    errors, scales = [], []
    for b in range(NB):
        block = jnp.where(upper == left, mat[b, b], 0.0)
        middle = jnp.where(identity, block, 0.0)
        row = lax.rsqrt(jnp.sum(middle, axis=0, keepdims=True))
        column = lax.rsqrt(jnp.sum(middle, axis=1, keepdims=True))
        block = block * row * column
        bound = jnp.max(jnp.sum(jnp.abs(block), axis=1, keepdims=True), axis=0, keepdims=True)
        errors.append(one - block / bound)
        scales.append(row * column / bound)

    def times(rows, square):
        (top, rest), (hi, lo) = split2(rows), split2(square)
        both = jnp.dot(top, hi, preferred_element_type=jnp.float32)
        both = both + jnp.dot(rest, hi, preferred_element_type=jnp.float32)
        return both + jnp.dot(top, lo, preferred_element_type=jnp.float32)

    sums = [one + error for error in errors]
    errors = [times(error, error) for error in errors]
    for n in range(DOUBLINGS):
        for b in range(NB):
            if n + 1 == DOUBLINGS:
                sums[b] = sums[b] + times(sums[b], errors[b])
            else:
                both = times(jnp.concatenate([errors[b], sums[b]], axis=0), errors[b])
                errors[b] = both[:B]
                sums[b] = sums[b] + both[B:]
    for b in range(NB):
        inverse[b] = sums[b] * scales[b]


def eliminate(mat, spare, right, columns, out):
    spare[...] = mat[...]
    spread_columns(right, columns)
    lane = lax.broadcasted_iota(jnp.int32, (B, B), 1)
    line = lax.broadcasted_iota(jnp.int32, (B, B), 0)

    def pivot(k, carry):
        kb, kr = k // B, k % B
        rows = [spare[kb, j, pl.ds(kr, 1), :] for j in range(NB)]
        entry = columns[kb, pl.ds(kr, 1), :]
        value = jnp.sum(jnp.where(lane[:1] == kr, spare[kb, kb, pl.ds(kr, 1), :], 0.0), axis=1, keepdims=True)

        def sweep(i, carry):
            factor = jnp.sum(jnp.where(lane == kr, spare[i, kb], 0.0), axis=1, keepdims=True) / value
            factor = jnp.where((line == kr) & (i == kb), 0.0, factor)
            for j in range(NB):
                spare[i, j] = spare[i, j] - factor * rows[j]
            columns[i] = columns[i] - factor * entry
            return carry

        return lax.fori_loop(0, NB, sweep, carry)

    lax.fori_loop(0, NC, pivot, 0)
    rows = []
    for b in range(NB):
        scale = jnp.sum(jnp.where(diagonal(), spare[b, b], 0.0), axis=1, keepdims=True)
        rows.append(to_row(columns[b] / scale))
    out[...] = pack(rows)


def first_steps(mat, inverse, columns, right):
    zero = jnp.zeros((NB, B), jnp.float32)
    pre = apply_diag(inverse, right, columns)
    size = dot(right, pre)
    bound = (TOL * TOL) * size
    image = apply_full(mat, columns)

    def advance(_, carry):
        res, pre, image, step, moved, total, size, ratio, length = carry
        step = pre + ratio * step
        moved = image + ratio * moved
        total = total + length * step
        res = res - length * moved
        pre = apply_diag(inverse, res, columns)
        latest = dot(res, pre)
        image = apply_full(mat, columns)
        active = latest > bound
        ratio = jnp.where(active, latest / size, 0.0)
        further = jnp.where(active, latest / (dot(image, pre) - ratio * latest / length), 0.0)
        return res, pre, image, step, moved, total, latest, ratio, further

    def finish(carry):
        _, pre, _, step, _, total, _, ratio, length = carry
        return total + length * (pre + ratio * step)

    start = (right, pre, image, zero, zero, zero, size, jnp.zeros((1, 1), jnp.float32), size / dot(image, pre))
    return advance, finish, start


def solve(mat, inverse, spare, columns, right, out, given=None, least=0.0):
    zero = jnp.zeros((NB, B), jnp.float32)

    def inner(res, pre, size, bound):
        image = apply_full(mat, columns)

        def going(carry):
            return (carry[0] < LIMIT) & (carry[1] > bound)

        def advance(carry):
            count, _, res, pre, image, step, moved, total, size, ratio, length = carry
            step = pre + ratio * step
            moved = image + ratio * moved
            total = total + length * step
            res = res - length * moved
            pre = apply_diag(inverse, res, columns)
            latest = dot(res, pre)
            image = apply_full(mat, columns)
            ratio = latest / size
            length = latest / (dot(image, pre) - ratio * latest / length)
            return count + 1, latest[0, 0], res, pre, image, step, moved, total, latest, ratio, length

        start = (
            jnp.int32(0), size[0, 0], res, pre, image, zero, zero, zero,
            size, jnp.zeros((1, 1), jnp.float32), size / dot(image, pre),
        )
        return lax.while_loop(going, advance, start)[7]

    def residual(value):
        spread_columns(value, columns)
        res = right - apply_full(mat, columns)
        pre = apply_diag(inverse, res, columns)
        return res, pre, dot(res, pre)

    pre = apply_diag(inverse, right, columns)
    whole = dot(right, pre)
    first = jnp.maximum(whole[0, 0], least)
    if given is None:
        out[...] = zero
        begun = (jnp.int32(0), whole[0, 0], right, pre, whole)
    else:
        out[...], res = given
        pre = apply_diag(inverse, res, columns)
        size = dot(res, pre)
        begun = (jnp.int32(0), size[0, 0], res, pre, size)

    def unsolved(carry):
        return (carry[0] < ROUNDS) & (carry[1] > CHECK * CHECK * first)

    def improve(carry):
        count, _, res, pre, size = carry
        out[...] += inner(res, pre, size, TOL * TOL * first)
        res, pre, size = residual(out[...])
        return count + 1, size[0, 0], res, pre, size

    final = lax.while_loop(unsolved, improve, begun)[1]

    @pl.when(jnp.logical_not(final <= CHECK * CHECK * first))
    def _():
        eliminate(mat, spare, right, columns, out)

    return first


def corner_fixed(block):
    low = lax.broadcasted_iota(jnp.int32, (B, B), 0) >= BLK
    low = low & (lax.broadcasted_iota(jnp.int32, (B, B), 1) < BLK)
    return jnp.where(low, block.T, block)


def right_side(grams):
    left = lax.broadcasted_iota(jnp.int32, (1, B), 1) < BLK
    sides = []
    for j in range(NB):
        even = grams[BLK + 2 * j : BLK + 2 * j + 1, :]
        odd = grams[BLK + 2 * j + 1 : BLK + 2 * j + 2, :]
        sides.append(jnp.where(left, even, pltpu.roll(odd, BLK, 1)))
    return pack(sides)


def unpack(ridge, grams, mat, core):
    identity = diagonal()
    for n in range(PER_CORE):
        block = grams[pl.ds(pl.multiple_of(core * HALF + n * B, B), B), :]
        if n == 0:
            block = corner_fixed(block)
        if n < 16:
            i, d = 4 * core + n // 4, n % 4
        else:
            i, d = 6 * core + n - 16, 4
        j = (i + d) % NB
        if d == 0:
            mat[i, i] = block + jnp.where(identity, ridge, 0.0)
        else:
            mat[i, j] = block
            mat[j, i] = block.T


def apply_operator(blocks, ridge, vector, columns):
    spread_columns(vector, columns)
    down = [jnp.zeros((8, B), jnp.float32)] * NB
    rows = []
    for i in range(NB):
        column = columns[i]
        across = jnp.zeros((B, B), jnp.float32)
        for j in range(NB):
            if (i, j) in INDEX:
                block = blocks[INDEX[i, j]]
                down[j] = down[j] + block_rows(block, column)
                if j != i:
                    across = across + block * vector[j : j + 1, :]
        rows.append(to_row(jnp.sum(across, axis=1, keepdims=True)))
    total = [jnp.sum(part, axis=0, keepdims=True) + row for part, row in zip(down, rows)]
    return pack(total) + ridge * vector


def solver_kernel(ridge, blocks, dense_t, mat, inverse, side, begin, left, solution, fitted, spare, columns, first, second):
    g = side[...]
    least = solve(mat, inverse, spare, columns, g, first, (begin[...], left[...]))
    z = first[...]
    h = apply_operator(blocks, ridge, z, columns)
    gain = dot(g, z)
    length = gain / dot(z, h)
    rest = g - length * h
    solve(mat, inverse, spare, columns, rest, second, least=least)
    s = second[...]
    latest = dot(rest, s)
    ratio = latest / gain
    image = apply_operator(blocks, ridge, s, columns) + ratio * h
    step = s + ratio * z
    curve = dot(step, image)
    x = length * z + jnp.where(curve > 0.0, latest / curve, 0.0) * step
    solution[...] = x

    spread_columns(x, columns)
    for half in range(2):
        acc = jnp.zeros((8, B), jnp.float32)
        for j in range(NB):
            part = dense_t[j * B : (j + 1) * B, half * B : (half + 1) * B].astype(jnp.float32)
            acc = acc + block_rows(part, columns[j])
        fitted[half : half + 1, :] = jnp.sum(acc, axis=0, keepdims=True)


def space(*shape):
    return pltpu.VMEM(shape, jnp.float32)


def shaped(*shape):
    return jax.ShapeDtypeStruct(shape, jnp.float32)


WHOLE = pl.BlockSpec(memory_space=pltpu.VMEM)
LIMITS = dict(vmem_limit_bytes=32 << 20)


def body(values, pattern, targets, root_weights):
    tiles = values.shape[0]
    own_rows = tiles * BLK
    rows_total = own_rows * lax.axis_size("rows") * lax.axis_size("grp")
    ridge = rows_total / (2.0 * NC)
    groups = 3 + 2 + 3 + 2 + 3 + 3
    job_space = [
        space(HALF, B),
        space(NZ - 1, SLAB, B),
        space(NY - 1, SLAB, B),
        space(NX - 1, WIDE, B),
        space(NY, CELL + THIN1, B),
        space(NZ, CELL + THIN2, B),
        space(NY - 1, CELL + THIN1, B),
        space(NZ - 1, CELL + THIN2, B),
        space(NX, 2 * CELL, B),
        space(NZ, THIN1, B),
        space(NY, THIN2, B),
        space(NY, CELL + THIN1, B),
        space(NZ, CELL + THIN2, B),
    ] + [pltpu.SemaphoreType.DMA((groups,))] * 2
    operator, dense_t, mat, inverse, side, begin, left = pl.pallas_call(
        lambda *refs: reduce_kernel(ridge, *refs),
        out_shape=(
            shaped(2 * HALF, B),
            jax.ShapeDtypeStruct((NC, own_rows), jnp.bfloat16),
            shaped(NB, NB, B, B),
            shaped(NB, B, B),
            shaped(NB, B),
            shaped(NB, B),
            shaped(NB, B),
        ),
        in_specs=[pl.BlockSpec(memory_space=pltpu.HBM)] * 4,
        out_specs=(WHOLE,) * 7,
        scratch_shapes=[
            pltpu.VMEM((2, B, WIDTH), jnp.bfloat16),
            pltpu.VMEM(pattern.shape, jnp.int32),
            space(1, WIDTH),
            space(1, WIDTH),
            space(2, B, WIDTH),
            space(8, WIDTH),
            space(2, B, WIDTH),
            space(8, WIDTH),
            pltpu.VMEM((NC + NC // 2, 2 * WIDTH), jnp.bfloat16),
            space(2 * HALF, B),
            space(NB, B, B),
            pltpu.SemaphoreType.DMA((4,)),
            pltpu.SemaphoreType.DMA((2,)),
            pltpu.SemaphoreType.DMA((2,)),
        ]
        + job_space * 2,
        compiler_params=pltpu.CompilerParams(collective_id=0, has_side_effects=True, **LIMITS),
    )(
        *(
            pltpu.with_memory_space_constraint(operand, pltpu.HBM)
            for operand in (
                values.reshape(tiles // 2, 2 * BLK, WIDTH), pattern, targets.reshape(1, -1), root_weights.reshape(1, -1)
            )
        )
    )
    solution_rows, fitted = pl.pallas_call(
        lambda *refs: solver_kernel(ridge, *refs),
        out_shape=(shaped(NB, B), shaped(own_rows // B, B)),
        in_specs=[WHOLE] * 7,
        out_specs=(WHOLE,) * 2,
        scratch_shapes=[space(NB, NB, B, B), space(NB, B, B), space(NB, B), space(NB, B)],
        compiler_params=pltpu.CompilerParams(**LIMITS),
    )(operator.reshape(len(PAIRS), B, B), dense_t, mat, inverse, side, begin, left)
    return solution_rows.reshape(-1), fitted.reshape(-1)


def solution(mesh):
    in_specs = (
        P(("rows", "grp"), None, None),
        P(("rows", "grp"), None),
        P(("rows", "grp")),
        P(("rows", "grp")),
    )
    out_specs = (P(), P(("rows", "grp")))
    return jax.shard_map(body, mesh=mesh, in_specs=in_specs, out_specs=out_specs, check_vma=False)
```

```python
import jax
import jax.numpy as jnp
from jax import lax
from jax.experimental import pallas as pl
from jax.experimental.pallas import tpu as pltpu
from jax.sharding import PartitionSpec as P

NC = 1024
BLK = 64
KB = 4
B = 128
NB = NC // B
WIDTH = KB * BLK
TOL = 5e-6
CHECK = 2e-5
LIMIT = 300
ROUNDS = 4
DOUBLINGS = 5
STEPS = 8
CONTRACT_LANES = (((1,), (1,)), ((), ()))
MESH = pl.DeviceIdType.MESH

NEAR = [(i, d) for i in range(NB // 2) for d in range(NB // 2)]
PAIRS = [(4 * c + i, (4 * c + i + d) % NB) for c in range(2) for i, d in NEAR]
PAIRS = PAIRS[:16] + [(0, 4), (1, 5)] + PAIRS[16:] + [(6, 2), (7, 3)]
PER_CORE = len(PAIRS) // 2
INDEX = {pair: n for n, pair in enumerate(PAIRS)}

NZ, NY, NX = 8, 8, 4
HALF = PER_CORE * B
PART_A, PART_B, PART_C = 0, 512, 1024
SLAB = 512 // NZ
CELL = SLAB // NY
WIDE = (HALF - PART_C) // NX
SIDE = 192
THIN1 = SIDE // NY
THIN2 = (WIDE - SIDE) // NZ


def split2(x):
    hi = x.astype(jnp.bfloat16)
    return hi, (x - hi.astype(jnp.float32)).astype(jnp.bfloat16)


def split3(x):
    hi = x.astype(jnp.bfloat16)
    mid, lo = split2(x - hi.astype(jnp.float32))
    return hi, mid, lo


def dot_nt(x, y):
    return lax.dot_general(x, y, CONTRACT_LANES, preferred_element_type=jnp.float32)


def stacked(row):
    parts = [part.astype(jnp.float32) for part in split3(row)]
    line = lax.broadcasted_iota(jnp.int32, (16, row.shape[1]), 0)
    value = jnp.where(line == 0, parts[0], 0.0)
    value = jnp.where(line == 1, parts[1], value)
    return jnp.where(line == 2, parts[2], value).astype(jnp.bfloat16)


def pack(rows):
    line = lax.broadcasted_iota(jnp.int32, (NB, B), 0)
    value = jnp.where(line == 0, rows[0], 0.0)
    for j in range(1, NB):
        value = jnp.where(line == j, rows[j], value)
    return value


def dense_block(values, columns, dense_t, lanes):
    rows = lax.broadcasted_iota(jnp.int32, (NC, WIDTH), 0).astype(jnp.float32)
    first = lax.broadcasted_iota(jnp.int32, (NC, B), 1) < BLK
    for half in range(2):
        pair = values[half].astype(jnp.bfloat16)
        picks = [
            jnp.where(rows == columns[n : n + 1, :], 1.0, 0.0).astype(jnp.bfloat16)
            for n in (2 * half, 2 * half + 1)
        ]
        both = jnp.where(first, dot_nt(picks[0], pair), dot_nt(picks[1], pair))
        start = lanes + half * B
        dense_t[:NC, start : start + B] = both.astype(jnp.bfloat16)


def remote(src, dst, send, recv, device):
    moved = pltpu.make_async_remote_copy(
        src_ref=src, dst_ref=dst, send_sem=send, recv_sem=recv, device_id=device, device_id_type=MESH
    )
    moved.start()
    return moved


def greet(peers):
    barrier = pltpu.get_barrier_semaphore()
    for peer in peers:
        pl.semaphore_signal(barrier, inc=1, device_id=peer, device_id_type=MESH)
    return barrier


def position():
    place = lax.axis_index("rows")
    return place, lax.axis_index("grp"), place % 2, (place // 2) % NY, place // (2 * NY)


def reduce_kernel(
    ridge, values_in, pattern_in, targets_in, weights_in, operator, own_dense, mat, inverse, side, begin, left,
    values, pattern, targets, weights, raw, extra, there, extra_there, dense_t, gathered_m, columns, load_sem,
    send_raw, recv_raw, *rest,
):
    place, x, core, y, z = position()
    loads = [
        pltpu.make_async_copy(source, target, load_sem.at[n])
        for n, (source, target) in enumerate(
            ((values_in, values), (pattern_in, pattern), (targets_in, targets), (weights_in, weights))
        )
    ]
    for item in loads:
        item.start()

    def along_z(d):
        return (((z + d) % NZ) * 2 * NY + y * 2 + core, x)

    def along_y(d):
        return (z * 2 * NY + ((y + d) % NY) * 2 + core, x)

    def along_x(d):
        return (place, (x + d) % NX)

    sibling = (place + 1 - 2 * core, x)
    peers = [sibling]
    peers += [along_z(d) for d in range(1, NZ)] + [along_y(d) for d in range(1, NY)]
    peers += [along_x(d) for d in range(1, NX)]
    barrier = greet(peers)
    for item in loads:
        item.wait()
    raw[...] = values[...].astype(jnp.float32)
    lane = lax.broadcasted_iota(jnp.int32, (1, WIDTH), 1)
    for n in range(4):
        block = jnp.where(lane < BLK, pattern[n : n + 1, 0:1], pattern[n : n + 1, 1:2])
        after = jnp.where(lane < 3 * BLK, pattern[n : n + 1, 2:3], pattern[n : n + 1, 3:4])
        block = jnp.where(lane < 2 * BLK, block, after)
        extra[n : n + 1, :] = (block * BLK + lane % BLK).astype(jnp.float32)
    square = weights[...] * weights[...]
    extra[4:5, :] = square
    extra[5:6, :] = square * targets[...]
    extra[6:8, :] = jnp.zeros((2, WIDTH), jnp.float32)
    pl.semaphore_wait(barrier, len(peers))

    first = remote(raw, there, send_raw.at[0], recv_raw.at[0], sibling)
    second = remote(extra, extra_there, send_raw.at[1], recv_raw.at[1], sibling)
    dense_block(values, extra, dense_t, 0)
    own_dense[...] = dense_t[:NC, :WIDTH]
    first.wait()
    second.wait()
    dense_block(there, extra_there, dense_t, WIDTH)

    dense_t[NC:, :] = dense_t[: NC // 2, :]
    own = 4 * core

    def near_blocks(local, product, which):
        for i in which:
            start = pl.multiple_of((own + i) * B, B)
            block = product(start, start, 4 * B)
            for d in range(4):
                row = (4 * i + d) * B
                local[row : row + B, :] = block[:, d * B : (d + 1) * B]

    def far_blocks(local, product):
        for i in range(2):
            start = pl.multiple_of((6 * core + i) * B, B)
            row = (16 + i) * B
            local[row : row + B, :] = product(start, pl.multiple_of(start + 4 * B, B), B)

    def plain(first, second, count):
        return dot_nt(dense_t[pl.ds(first, B), :], dense_t[pl.ds(second, count), :])

    square = jnp.concatenate([extra[4:5, :], extra_there[4:5, :]], axis=1)

    def weighted(first, second, count):
        hi, lo = split2(dense_t[pl.ds(first, B), :].astype(jnp.float32) * square)
        others = dense_t[pl.ds(second, count), :]
        return dot_nt(hi, others) + dot_nt(lo, others)

    def rows(start, count):
        return pl.ds(pl.multiple_of(start, 8), count)

    def total(mine, arrived):
        value = mine
        for n in range(arrived.shape[0]):
            value = value + arrived[n]
        return value

    def ordered(slots):
        value = slots[0]
        for n in range(1, slots.shape[0]):
            value = value + slots[n]
        return value

    def settle(ref, sem):
        pltpu.make_async_copy(ref, ref, sem).wait()

    def scatter(axis, piece, landing, send, recv):
        step, me, size = axis
        for d in range(1, size):
            remote(piece((me + d) % size), landing.at[d - 1], send, recv, step(d))

    def spread(axis, block, send, recv):
        step, _, size = axis
        for d in range(1, size):
            remote(block, block, send, recv, step(d))

    axis_z, axis_y, axis_x = (along_z, z, NZ), (along_y, y, NY), (along_x, x, NX)
    half = core * HALF

    def job(refs, result, product, finish, late):
        local, in_a, in_b, in_c, relay, pass_on, mix_y, mix_z, in_y, in_z, in_cells, in_thin1, in_thin2, out_y, out_z, send, recv = refs
        sizes = []

        def sems(count):
            sizes.append(count)
            return send.at[len(sizes) - 1], recv.at[len(sizes) - 1]

        def place_of(start, count):
            return result.at[rows(half + start, count)]

        def part(start, count):
            return lambda k: local.at[rows(start + k * count, count)]

        def opposite():
            out = [sems(WIDE // 2) for _ in range(4)]
            left, right, across = (x + NX - 1) % NX, (x + 1) % NX, (x + 2) % NX
            middle = WIDE // 2
            far = PART_C + across * WIDE
            remote(local.at[rows(far, middle)], relay.at[0], *out[0], along_x(1))
            remote(local.at[rows(far + middle, middle)], relay.at[1], *out[1], along_x(NX - 1))
            near = PART_C + right * WIDE + middle
            remote(local.at[rows(near, middle)], in_c.at[0, pl.ds(middle, middle)], *out[2], along_x(1))
            near = PART_C + left * WIDE
            remote(local.at[rows(near, middle)], in_c.at[1, pl.ds(0, middle)], *out[3], along_x(NX - 1))
            return out

        def relayed(out):
            left, right, middle = (x + NX - 1) % NX, (x + 1) % NX, WIDE // 2
            more = [sems(middle) for _ in range(2)]
            settle(relay.at[0], out[0][1])
            pass_on[0] = relay[0] + local[rows(PART_C + right * WIDE, middle), :]
            remote(pass_on.at[0], in_c.at[0, pl.ds(0, middle)], *more[0], along_x(1))
            settle(relay.at[1], out[1][1])
            pass_on[1] = relay[1] + local[rows(PART_C + left * WIDE + middle, middle), :]
            remote(pass_on.at[1], in_c.at[1, pl.ds(middle, middle)], *more[1], along_x(NX - 1))
            return out[2:] + more

        if late:
            near_blocks(local, product, (0, 1, 2, 3))
            far_blocks(local, product)
            finish(local)
            yield
            by_x = opposite()
            sem_b = sems((NY - 1) * SLAB)
            scatter(axis_y, part(PART_B, SLAB), in_b, *sem_b)
        else:
            near_blocks(local, product, (2, 3))
            far_blocks(local, product)
            by_x = opposite()
            near_blocks(local, product, (1,))
            sem_b = sems((NY - 1) * SLAB)
            scatter(axis_y, part(PART_B, SLAB), in_b, *sem_b)
            near_blocks(local, product, (0,))
            finish(local)
        sem_a = sems((NZ - 1) * SLAB)
        scatter(axis_z, part(PART_A, SLAB), in_a, *sem_a)
        yield
        by_x = relayed(by_x)
        yield
        settle(in_a, sem_a[1])
        slab = total(local[rows(PART_A + z * SLAB, SLAB), :], in_a)
        for k in range(NY):
            mix_y[k, :CELL, :] = slab[k * CELL : (k + 1) * CELL]
        settle(in_b, sem_b[1])
        slab = total(local[rows(PART_B + y * SLAB, SLAB), :], in_b)
        for k in range(NZ):
            mix_z[k, :CELL, :] = slab[k * CELL : (k + 1) * CELL]
        for n, pair in enumerate(by_x):
            settle(relay.at[n % 2], pair[1])
        slab = total(local[rows(PART_C + x * WIDE, WIDE), :], in_c)
        for k in range(NY):
            mix_y[k, CELL:, :] = slab[k * THIN1 : (k + 1) * THIN1]
        for k in range(NZ):
            mix_z[k, CELL:, :] = slab[SIDE + k * THIN2 : SIDE + (k + 1) * THIN2]
        sem_y, sem_z = sems((NY - 1) * (CELL + THIN1)), sems((NZ - 1) * (CELL + THIN2))
        scatter(axis_y, lambda k: mix_y.at[k], in_y, *sem_y)
        scatter(axis_z, lambda k: mix_z.at[k], in_z, *sem_z)
        yield
        settle(in_y, sem_y[1])
        mixed = total(mix_y[y], in_y)
        in_cells[x, :CELL, :] = mixed[:CELL]
        in_thin1[z] = mixed[CELL:]
        sem_1 = sems((NZ - 1) * THIN1)
        spread(axis_z, in_thin1.at[z], *sem_1)
        settle(in_z, sem_z[1])
        mixed = total(mix_z[z], in_z)
        in_cells[x, CELL:, :] = mixed[:CELL]
        in_thin2[y] = mixed[CELL:]
        sem_2, sem_3 = sems((NY - 1) * THIN2), sems((NX - 1) * 2 * CELL)
        spread(axis_y, in_thin2.at[y], *sem_2)
        spread(axis_x, in_cells.at[x], *sem_3)
        yield
        settle(in_cells.at[pl.ds(0, NX - 1)], sem_3[1])
        both = ordered(in_cells)
        settle(in_thin1.at[pl.ds(0, NZ - 1)], sem_1[1])
        out_y[y, :CELL, :] = both[:CELL]
        out_y[y, CELL:, :] = ordered(in_thin1)
        sem_y = sems((NY - 1) * (CELL + THIN1))
        spread(axis_y, out_y.at[y], *sem_y)
        settle(in_thin2.at[pl.ds(0, NY - 1)], sem_2[1])
        out_z[z, :CELL, :] = both[CELL:]
        out_z[z, CELL:, :] = ordered(in_thin2)
        sem_z = sems((NZ - 1) * (CELL + THIN2))
        spread(axis_z, out_z.at[z], *sem_z)
        yield
        big_a, big_b = place_of(PART_A + z * SLAB, SLAB), place_of(PART_B + y * SLAB, SLAB)
        big_c = place_of(PART_C + x * WIDE, WIDE)
        settle(out_y.at[pl.ds(0, NY - 1)], sem_y[1])
        settle(out_z.at[pl.ds(0, NZ - 1)], sem_z[1])
        big_c[:SIDE, :] = out_y[:, CELL:, :].reshape(SIDE, B)
        big_c[SIDE:, :] = out_z[:, CELL:, :].reshape(WIDE - SIDE, B)
        middle = WIDE // 2
        firsts, seconds = [sems(middle) for _ in range(2)], [sems(middle) for _ in range(2)]
        upper, lower = place_of(PART_C + x * WIDE, middle), place_of(PART_C + x * WIDE + middle, middle)
        remote(upper, upper, *firsts[0], along_x(1))
        remote(lower, lower, *firsts[1], along_x(NX - 1))
        remote(lower, lower, *seconds[0], along_x(1))
        remote(upper, upper, *seconds[1], along_x(NX - 1))
        big_a[...] = out_y[:, :CELL, :].reshape(SLAB, B)
        sem_a = sems((NZ - 1) * SLAB)
        spread(axis_z, big_a, *sem_a)
        big_b[...] = out_z[:, :CELL, :].reshape(SLAB, B)
        sem_b = sems((NY - 1) * SLAB)
        spread(axis_y, big_b, *sem_b)
        yield
        forward = [sems(middle) for _ in range(2)]
        from_left = place_of(PART_C + ((x + NX - 1) % NX) * WIDE, middle)
        from_right = place_of(PART_C + ((x + 1) % NX) * WIDE + middle, middle)
        settle(from_left, firsts[0][1])
        remote(from_left, from_left, *forward[0], along_x(1))
        settle(from_right, firsts[1][1])
        remote(from_right, from_right, *forward[1], along_x(NX - 1))
        yield
        across = []
        for start, count, size, waits in (
            (PART_A, PART_B - PART_A, (NZ - 1) * SLAB, [sem_a]),
            (PART_B, PART_C - PART_B, (NY - 1) * SLAB, [sem_b]),
            (PART_C, HALF - PART_C, middle, seconds + forward),
        ):
            for _, arrived in waits:
                settle(local.at[pl.ds(0, size)], arrived)
            pair = sems(count)
            block = place_of(start, count)
            remote(block, block, *pair, sibling)
            across.append((block, pair[1]))
        yield
        for block, arrived in across:
            settle(block, arrived)
        yield
        for n, moved in enumerate(sizes):
            settle(local.at[pl.ds(0, moved)], send.at[n])
        yield

    count = len(rest) // 2
    locals_m, locals_w = rest[:count], rest[count:]
    aims = stacked(jnp.concatenate([extra[5:6, :], extra_there[5:6, :]], axis=1))

    def add_side(local):
        for c in range(NC // BLK):
            line = dot_nt(aims, dense_t[c * BLK : (c + 1) * BLK, :])
            local[BLK + c : BLK + c + 1, :BLK] = jnp.sum(line, axis=0, keepdims=True)

    job_m = job(locals_m, gathered_m, plain, add_side, False)
    job_w = job(locals_w, operator, weighted, lambda local: None, True)
    for turn in "mwmww" + "mw" * 3 + "mmwmw":
        next(job_m if turn == "m" else job_w)
    unpack(ridge, gathered_m, mat, core)
    invert_blocks(mat, inverse, 4 * core)
    next(job_m)
    unpack(ridge, gathered_m, mat, 1 - core)
    side[...] = right_side(gathered_m)

    invert_blocks(mat, inverse, 4 - 4 * core)
    advance, finish, state = first_steps(mat, inverse, columns, side[...])
    state = lax.fori_loop(0, 2, advance, state)
    next(job_w)
    state = lax.fori_loop(2, STEPS - 1, advance, state)
    value = finish(state)
    begin[...] = value
    spread_columns(value, columns)
    left[...] = side[...] - apply_full(mat, columns)
    next(job_w)
    next(job_m)
    next(job_w)


def diagonal():
    shape = (B, B)
    return lax.broadcasted_iota(jnp.int32, shape, 0) == lax.broadcasted_iota(jnp.int32, shape, 1)


def to_row(column):
    return jnp.sum(jnp.where(diagonal(), column, 0.0), axis=0, keepdims=True)


def to_column(row):
    return jnp.sum(jnp.where(diagonal(), row, 0.0), axis=1, keepdims=True)


def dot(x, y):
    return jnp.sum(jnp.sum(x * y, axis=0, keepdims=True), axis=1, keepdims=True)


def block_rows(block, column):
    return jnp.sum((block * column).reshape(B // 8, 8, B), axis=0)


def spread_columns(vector, columns):
    for j in range(NB):
        columns[j] = jnp.broadcast_to(to_column(vector[j : j + 1, :]), (B, B))


def apply_full(mat, columns):
    acc = [None] * NB
    for i in range(NB):
        column = columns[i]
        for j in range(NB):
            part = block_rows(mat[i, j], column)
            acc[j] = part if acc[j] is None else acc[j] + part
    return pack([jnp.sum(part, axis=0, keepdims=True) for part in acc])


def apply_diag(inverse, vector, columns):
    rows = []
    for b in range(NB):
        column = jnp.sum(inverse[b] * vector[b : b + 1, :], axis=1, keepdims=True)
        column = jnp.broadcast_to(column, (B, B))
        columns[b] = column
        rows.append(to_row(column))
    return pack(rows)


def invert_blocks(mat, inverse, start):
    identity = diagonal()
    one = jnp.where(identity, 1.0, 0.0)
    upper = lax.broadcasted_iota(jnp.int32, (B, B), 0) < BLK
    left = lax.broadcasted_iota(jnp.int32, (B, B), 1) < BLK
    errors, scales = [], []
    for b in range(NB // 2):
        block = jnp.where(upper == left, mat[start + b, start + b], 0.0)
        middle = jnp.where(identity, block, 0.0)
        row = lax.rsqrt(jnp.sum(middle, axis=0, keepdims=True))
        column = lax.rsqrt(jnp.sum(middle, axis=1, keepdims=True))
        block = block * row * column
        bound = jnp.max(jnp.sum(jnp.abs(block), axis=1, keepdims=True), axis=0, keepdims=True)
        errors.append(one - block / bound)
        scales.append(row * column / bound)

    def times(rows, square):
        (top, rest), (hi, lo) = split2(rows), split2(square)
        both = jnp.dot(top, hi, preferred_element_type=jnp.float32)
        both = both + jnp.dot(rest, hi, preferred_element_type=jnp.float32)
        return both + jnp.dot(top, lo, preferred_element_type=jnp.float32)

    sums = [one + error for error in errors]
    errors = [times(error, error) for error in errors]
    for n in range(DOUBLINGS):
        for b in range(NB // 2):
            if n + 1 == DOUBLINGS:
                sums[b] = sums[b] + times(sums[b], errors[b])
            else:
                both = times(jnp.concatenate([errors[b], sums[b]], axis=0), errors[b])
                errors[b] = both[:B]
                sums[b] = sums[b] + both[B:]
    for b in range(NB // 2):
        inverse[start + b] = sums[b] * scales[b]


def eliminate(mat, spare, right, columns, out):
    spare[...] = mat[...]
    spread_columns(right, columns)
    lane = lax.broadcasted_iota(jnp.int32, (B, B), 1)
    line = lax.broadcasted_iota(jnp.int32, (B, B), 0)

    def pivot(k, carry):
        kb, kr = k // B, k % B
        rows = [spare[kb, j, pl.ds(kr, 1), :] for j in range(NB)]
        entry = columns[kb, pl.ds(kr, 1), :]
        value = jnp.sum(jnp.where(lane[:1] == kr, spare[kb, kb, pl.ds(kr, 1), :], 0.0), axis=1, keepdims=True)

        def sweep(i, carry):
            factor = jnp.sum(jnp.where(lane == kr, spare[i, kb], 0.0), axis=1, keepdims=True) / value
            factor = jnp.where((line == kr) & (i == kb), 0.0, factor)
            for j in range(NB):
                spare[i, j] = spare[i, j] - factor * rows[j]
            columns[i] = columns[i] - factor * entry
            return carry

        return lax.fori_loop(0, NB, sweep, carry)

    lax.fori_loop(0, NC, pivot, 0)
    rows = []
    for b in range(NB):
        scale = jnp.sum(jnp.where(diagonal(), spare[b, b], 0.0), axis=1, keepdims=True)
        rows.append(to_row(columns[b] / scale))
    out[...] = pack(rows)


def first_steps(mat, inverse, columns, right):
    zero = jnp.zeros((NB, B), jnp.float32)
    pre = apply_diag(inverse, right, columns)
    size = dot(right, pre)
    bound = (TOL * TOL) * size
    image = apply_full(mat, columns)

    def advance(_, carry):
        res, pre, image, step, moved, total, size, ratio, length = carry
        step = pre + ratio * step
        moved = image + ratio * moved
        total = total + length * step
        res = res - length * moved
        pre = apply_diag(inverse, res, columns)
        latest = dot(res, pre)
        image = apply_full(mat, columns)
        active = latest > bound
        ratio = jnp.where(active, latest / size, 0.0)
        further = jnp.where(active, latest / (dot(image, pre) - ratio * latest / length), 0.0)
        return res, pre, image, step, moved, total, latest, ratio, further

    def finish(carry):
        _, pre, _, step, _, total, _, ratio, length = carry
        return total + length * (pre + ratio * step)

    start = (right, pre, image, zero, zero, zero, size, jnp.zeros((1, 1), jnp.float32), size / dot(image, pre))
    return advance, finish, start


def solve(mat, inverse, spare, columns, right, out, given=None, least=0.0):
    zero = jnp.zeros((NB, B), jnp.float32)

    def inner(res, pre, size, bound):
        image = apply_full(mat, columns)

        def going(carry):
            return (carry[0] < LIMIT) & (carry[1] > bound)

        def advance(carry):
            count, _, res, pre, image, step, moved, total, size, ratio, length = carry
            step = pre + ratio * step
            moved = image + ratio * moved
            total = total + length * step
            res = res - length * moved
            pre = apply_diag(inverse, res, columns)
            latest = dot(res, pre)
            image = apply_full(mat, columns)
            ratio = latest / size
            length = latest / (dot(image, pre) - ratio * latest / length)
            return count + 1, latest[0, 0], res, pre, image, step, moved, total, latest, ratio, length

        start = (
            jnp.int32(0), size[0, 0], res, pre, image, zero, zero, zero,
            size, jnp.zeros((1, 1), jnp.float32), size / dot(image, pre),
        )
        return lax.while_loop(going, advance, start)[7]

    def residual(value):
        spread_columns(value, columns)
        res = right - apply_full(mat, columns)
        pre = apply_diag(inverse, res, columns)
        return res, pre, dot(res, pre)

    pre = apply_diag(inverse, right, columns)
    whole = dot(right, pre)
    first = jnp.maximum(whole[0, 0], least)
    if given is None:
        out[...] = zero
        begun = (jnp.int32(0), whole[0, 0], right, pre, whole)
    else:
        out[...], res = given
        pre = apply_diag(inverse, res, columns)
        size = dot(res, pre)
        begun = (jnp.int32(0), size[0, 0], res, pre, size)

    def unsolved(carry):
        return (carry[0] < ROUNDS) & (carry[1] > CHECK * CHECK * first)

    def improve(carry):
        count, _, res, pre, size = carry
        out[...] += inner(res, pre, size, TOL * TOL * first)
        res, pre, size = residual(out[...])
        return count + 1, size[0, 0], res, pre, size

    final = lax.while_loop(unsolved, improve, begun)[1]

    @pl.when(jnp.logical_not(final <= CHECK * CHECK * first))
    def _():
        eliminate(mat, spare, right, columns, out)

    return first


def corner_fixed(block):
    low = lax.broadcasted_iota(jnp.int32, (B, B), 0) >= BLK
    low = low & (lax.broadcasted_iota(jnp.int32, (B, B), 1) < BLK)
    return jnp.where(low, block.T, block)


def right_side(grams):
    left = lax.broadcasted_iota(jnp.int32, (1, B), 1) < BLK
    sides = []
    for j in range(NB):
        even = grams[BLK + 2 * j : BLK + 2 * j + 1, :]
        odd = grams[BLK + 2 * j + 1 : BLK + 2 * j + 2, :]
        sides.append(jnp.where(left, even, pltpu.roll(odd, BLK, 1)))
    return pack(sides)


def unpack(ridge, grams, mat, core):
    identity = diagonal()
    for n in range(PER_CORE):
        block = grams[pl.ds(pl.multiple_of(core * HALF + n * B, B), B), :]
        if n == 0:
            block = corner_fixed(block)
        if n < 16:
            i, d = 4 * core + n // 4, n % 4
        else:
            i, d = 6 * core + n - 16, 4
        j = (i + d) % NB
        if d == 0:
            mat[i, i] = block + jnp.where(identity, ridge, 0.0)
        else:
            mat[i, j] = block
            mat[j, i] = block.T


def apply_operator(blocks, ridge, vector, columns):
    spread_columns(vector, columns)
    down = [jnp.zeros((8, B), jnp.float32)] * NB
    rows = []
    for i in range(NB):
        column = columns[i]
        across = jnp.zeros((B, B), jnp.float32)
        for j in range(NB):
            if (i, j) in INDEX:
                block = blocks[INDEX[i, j]]
                down[j] = down[j] + block_rows(block, column)
                if j != i:
                    across = across + block * vector[j : j + 1, :]
        rows.append(to_row(jnp.sum(across, axis=1, keepdims=True)))
    total = [jnp.sum(part, axis=0, keepdims=True) + row for part, row in zip(down, rows)]
    return pack(total) + ridge * vector


def solver_kernel(ridge, blocks, dense_t, mat, inverse, side, begin, left, solution, fitted, spare, columns, first, second):
    g = side[...]
    least = solve(mat, inverse, spare, columns, g, first, (begin[...], left[...]))
    z = first[...]
    h = apply_operator(blocks, ridge, z, columns)
    gain = dot(g, z)
    length = gain / dot(z, h)
    rest = g - length * h
    solve(mat, inverse, spare, columns, rest, second, least=least)
    s = second[...]
    latest = dot(rest, s)
    ratio = latest / gain
    image = apply_operator(blocks, ridge, s, columns) + ratio * h
    step = s + ratio * z
    curve = dot(step, image)
    x = length * z + jnp.where(curve > 0.0, latest / curve, 0.0) * step
    solution[...] = x

    spread_columns(x, columns)
    for half in range(2):
        acc = jnp.zeros((8, B), jnp.float32)
        for j in range(NB):
            part = dense_t[j * B : (j + 1) * B, half * B : (half + 1) * B].astype(jnp.float32)
            acc = acc + block_rows(part, columns[j])
        fitted[half : half + 1, :] = jnp.sum(acc, axis=0, keepdims=True)


def space(*shape):
    return pltpu.VMEM(shape, jnp.float32)


def shaped(*shape):
    return jax.ShapeDtypeStruct(shape, jnp.float32)


WHOLE = pl.BlockSpec(memory_space=pltpu.VMEM)
LIMITS = dict(vmem_limit_bytes=32 << 20)


def body(values, pattern, targets, root_weights):
    tiles = values.shape[0]
    own_rows = tiles * BLK
    rows_total = own_rows * lax.axis_size("rows") * lax.axis_size("grp")
    ridge = rows_total / (2.0 * NC)
    groups = 8 + 2 + 3 + 2 + 8 + 3
    job_space = [
        space(HALF, B),
        space(NZ - 1, SLAB, B),
        space(NY - 1, SLAB, B),
        space(2, WIDE, B),
        space(2, WIDE // 2, B),
        space(2, WIDE // 2, B),
        space(NY, CELL + THIN1, B),
        space(NZ, CELL + THIN2, B),
        space(NY - 1, CELL + THIN1, B),
        space(NZ - 1, CELL + THIN2, B),
        space(NX, 2 * CELL, B),
        space(NZ, THIN1, B),
        space(NY, THIN2, B),
        space(NY, CELL + THIN1, B),
        space(NZ, CELL + THIN2, B),
    ] + [pltpu.SemaphoreType.DMA((groups,))] * 2
    operator, dense_t, mat, inverse, side, begin, left = pl.pallas_call(
        lambda *refs: reduce_kernel(ridge, *refs),
        out_shape=(
            shaped(2 * HALF, B),
            jax.ShapeDtypeStruct((NC, own_rows), jnp.bfloat16),
            shaped(NB, NB, B, B),
            shaped(NB, B, B),
            shaped(NB, B),
            shaped(NB, B),
            shaped(NB, B),
        ),
        in_specs=[pl.BlockSpec(memory_space=pltpu.HBM)] * 4,
        out_specs=(WHOLE,) * 7,
        scratch_shapes=[
            pltpu.VMEM((2, B, WIDTH), jnp.bfloat16),
            pltpu.VMEM(pattern.shape, jnp.int32),
            space(1, WIDTH),
            space(1, WIDTH),
            space(2, B, WIDTH),
            space(8, WIDTH),
            space(2, B, WIDTH),
            space(8, WIDTH),
            pltpu.VMEM((NC + NC // 2, 2 * WIDTH), jnp.bfloat16),
            space(2 * HALF, B),
            space(NB, B, B),
            pltpu.SemaphoreType.DMA((4,)),
            pltpu.SemaphoreType.DMA((2,)),
            pltpu.SemaphoreType.DMA((2,)),
        ]
        + job_space * 2,
        compiler_params=pltpu.CompilerParams(collective_id=0, has_side_effects=True, **LIMITS),
    )(
        *(
            pltpu.with_memory_space_constraint(operand, pltpu.HBM)
            for operand in (
                values.reshape(tiles // 2, 2 * BLK, WIDTH), pattern, targets.reshape(1, -1), root_weights.reshape(1, -1)
            )
        )
    )
    solution_rows, fitted = pl.pallas_call(
        lambda *refs: solver_kernel(ridge, *refs),
        out_shape=(shaped(NB, B), shaped(own_rows // B, B)),
        in_specs=[WHOLE] * 7,
        out_specs=(WHOLE,) * 2,
        scratch_shapes=[space(NB, NB, B, B), space(NB, B, B), space(NB, B), space(NB, B)],
        compiler_params=pltpu.CompilerParams(**LIMITS),
    )(operator.reshape(len(PAIRS), B, B), dense_t, mat, inverse, side, begin, left)
    return solution_rows.reshape(-1), fitted.reshape(-1)


def solution(mesh):
    in_specs = (
        P(("rows", "grp"), None, None),
        P(("rows", "grp"), None),
        P(("rows", "grp")),
        P(("rows", "grp")),
    )
    out_specs = (P(), P(("rows", "grp")))
    return jax.shard_map(body, mesh=mesh, in_specs=in_specs, out_specs=out_specs, check_vma=False)
```

```python
import jax
import jax.numpy as jnp
from jax import lax
from jax.experimental import pallas as pl
from jax.experimental.pallas import tpu as pltpu
from jax.sharding import PartitionSpec as P

NC = 1024
BLK = 64
KB = 4
B = 128
NB = NC // B
WIDTH = KB * BLK
TOL = 5e-6
CHECK = 2e-5
LIMIT = 300
ROUNDS = 4
DOUBLINGS = 5
STEPS = 8
CONTRACT_LANES = (((1,), (1,)), ((), ()))
MESH = pl.DeviceIdType.MESH

NEAR = [(i, d) for i in range(NB // 2) for d in range(NB // 2)]
PAIRS = [(4 * c + i, (4 * c + i + d) % NB) for c in range(2) for i, d in NEAR]
PAIRS = PAIRS[:16] + [(0, 4), (1, 5)] + PAIRS[16:] + [(6, 2), (7, 3)]
PER_CORE = len(PAIRS) // 2
INDEX = {pair: n for n, pair in enumerate(PAIRS)}

NZ, NY, NX = 8, 8, 4
HALF = PER_CORE * B
PART_A, PART_B, PART_C = 0, 512, 1024
SLAB = 512 // NZ
CELL = SLAB // NY
WIDE = (HALF - PART_C) // NX
SIDE = 192
THIN1 = SIDE // NY
THIN2 = (WIDE - SIDE) // NZ


def split2(x):
    hi = x.astype(jnp.bfloat16)
    return hi, (x - hi.astype(jnp.float32)).astype(jnp.bfloat16)


def split3(x):
    hi = x.astype(jnp.bfloat16)
    mid, lo = split2(x - hi.astype(jnp.float32))
    return hi, mid, lo


def dot_nt(x, y):
    return lax.dot_general(x, y, CONTRACT_LANES, preferred_element_type=jnp.float32)


def stacked(row):
    parts = [part.astype(jnp.float32) for part in split3(row)]
    line = lax.broadcasted_iota(jnp.int32, (16, row.shape[1]), 0)
    value = jnp.where(line == 0, parts[0], 0.0)
    value = jnp.where(line == 1, parts[1], value)
    return jnp.where(line == 2, parts[2], value).astype(jnp.bfloat16)


def pack(rows):
    line = lax.broadcasted_iota(jnp.int32, (NB, B), 0)
    value = jnp.where(line == 0, rows[0], 0.0)
    for j in range(1, NB):
        value = jnp.where(line == j, rows[j], value)
    return value


def dense_block(values, columns, dense_t, lanes):
    rows = lax.broadcasted_iota(jnp.int32, (NC, WIDTH), 0).astype(jnp.float32)
    first = lax.broadcasted_iota(jnp.int32, (NC, B), 1) < BLK
    for half in range(2):
        pair = values[half].astype(jnp.bfloat16)
        picks = [
            jnp.where(rows == columns[n : n + 1, :], 1.0, 0.0).astype(jnp.bfloat16)
            for n in (2 * half, 2 * half + 1)
        ]
        both = jnp.where(first, dot_nt(picks[0], pair), dot_nt(picks[1], pair))
        start = lanes + half * B
        dense_t[:NC, start : start + B] = both.astype(jnp.bfloat16)


def remote(src, dst, send, recv, device):
    moved = pltpu.make_async_remote_copy(
        src_ref=src, dst_ref=dst, send_sem=send, recv_sem=recv, device_id=device, device_id_type=MESH
    )
    moved.start()
    return moved


def greet(peers):
    barrier = pltpu.get_barrier_semaphore()
    for peer in peers:
        pl.semaphore_signal(barrier, inc=1, device_id=peer, device_id_type=MESH)
    return barrier


def position():
    place = lax.axis_index("rows")
    return place, lax.axis_index("grp"), place % 2, (place // 2) % NY, place // (2 * NY)


def reduce_kernel(
    ridge, values_in, pattern_in, targets_in, weights_in, operator, own_dense, mat, inverse, side, begin, left,
    values, pattern, targets, weights, raw, extra, there, extra_there, dense_t, gathered_m, columns, load_sem,
    send_raw, recv_raw, *rest,
):
    place, x, core, y, z = position()
    loads = [
        pltpu.make_async_copy(source, target, load_sem.at[n])
        for n, (source, target) in enumerate(
            ((values_in, values), (pattern_in, pattern), (targets_in, targets), (weights_in, weights))
        )
    ]
    for item in loads:
        item.start()

    def along_z(d):
        return (((z + d) % NZ) * 2 * NY + y * 2 + core, x)

    def along_y(d):
        return (z * 2 * NY + ((y + d) % NY) * 2 + core, x)

    def along_x(d):
        return (place, (x + d) % NX)

    sibling = (place + 1 - 2 * core, x)
    peers = [sibling]
    peers += [along_z(d) for d in range(1, NZ)] + [along_y(d) for d in range(1, NY)]
    peers += [along_x(d) for d in range(1, NX)]
    barrier = greet(peers)
    for item in loads:
        item.wait()
    raw[...] = values[...].astype(jnp.float32)
    lane = lax.broadcasted_iota(jnp.int32, (1, WIDTH), 1)
    for n in range(4):
        block = jnp.where(lane < BLK, pattern[n : n + 1, 0:1], pattern[n : n + 1, 1:2])
        after = jnp.where(lane < 3 * BLK, pattern[n : n + 1, 2:3], pattern[n : n + 1, 3:4])
        block = jnp.where(lane < 2 * BLK, block, after)
        extra[n : n + 1, :] = (block * BLK + lane % BLK).astype(jnp.float32)
    square = weights[...] * weights[...]
    extra[4:5, :] = square
    extra[5:6, :] = square * targets[...]
    extra[6:8, :] = jnp.zeros((2, WIDTH), jnp.float32)
    pl.semaphore_wait(barrier, len(peers))

    first = remote(raw, there, send_raw.at[0], recv_raw.at[0], sibling)
    second = remote(extra, extra_there, send_raw.at[1], recv_raw.at[1], sibling)
    dense_block(values, extra, dense_t, 0)
    own_dense[...] = dense_t[:NC, :WIDTH]
    first.wait()
    second.wait()
    dense_block(there, extra_there, dense_t, WIDTH)

    dense_t[NC:, :] = dense_t[: NC // 2, :]
    own = 4 * core

    def near_blocks(local, product, which):
        for i in which:
            start = pl.multiple_of((own + i) * B, B)
            block = product(start, start, 4 * B)
            for d in range(4):
                row = (4 * i + d) * B
                local[row : row + B, :] = block[:, d * B : (d + 1) * B]

    def far_blocks(local, product):
        for i in range(2):
            start = pl.multiple_of((6 * core + i) * B, B)
            row = (16 + i) * B
            local[row : row + B, :] = product(start, pl.multiple_of(start + 4 * B, B), B)

    def plain(first, second, count):
        return dot_nt(dense_t[pl.ds(first, B), :], dense_t[pl.ds(second, count), :])

    square = jnp.concatenate([extra[4:5, :], extra_there[4:5, :]], axis=1)

    def weighted(first, second, count):
        hi, lo = split2(dense_t[pl.ds(first, B), :].astype(jnp.float32) * square)
        others = dense_t[pl.ds(second, count), :]
        return dot_nt(hi, others) + dot_nt(lo, others)

    def rows(start, count):
        return pl.ds(pl.multiple_of(start, 8), count)

    def total(mine, arrived):
        value = mine
        for n in range(arrived.shape[0]):
            value = value + arrived[n]
        return value

    def ordered(slots):
        value = slots[0]
        for n in range(1, slots.shape[0]):
            value = value + slots[n]
        return value

    def settle(ref, sem):
        pltpu.make_async_copy(ref, ref, sem).wait()

    def scatter(axis, piece, landing, send, recv):
        step, me, size = axis
        for d in range(1, size):
            remote(piece((me + d) % size), landing.at[d - 1], send, recv, step(d))

    def spread(axis, block, send, recv):
        step, _, size = axis
        for d in range(1, size):
            remote(block, block, send, recv, step(d))

    axis_z, axis_y, axis_x = (along_z, z, NZ), (along_y, y, NY), (along_x, x, NX)
    half = core * HALF

    def job(refs, result, product, finish, late):
        local, in_a, in_b, in_c, relay, pass_on, mix_y, mix_z, in_y, in_z, in_cells, in_thin1, in_thin2, out_y, out_z, send, recv = refs
        sizes = []

        def sems(count):
            sizes.append(count)
            return send.at[len(sizes) - 1], recv.at[len(sizes) - 1]

        def place_of(start, count):
            return result.at[rows(half + start, count)]

        def part(start, count):
            return lambda k: local.at[rows(start + k * count, count)]

        def opposite():
            out = [sems(WIDE // 2) for _ in range(4)]
            left, right, across = (x + NX - 1) % NX, (x + 1) % NX, (x + 2) % NX
            middle = WIDE // 2
            far = PART_C + across * WIDE
            remote(local.at[rows(far, middle)], relay.at[0], *out[0], along_x(1))
            remote(local.at[rows(far + middle, middle)], relay.at[1], *out[1], along_x(NX - 1))
            near = PART_C + right * WIDE + middle
            remote(local.at[rows(near, middle)], in_c.at[0, pl.ds(middle, middle)], *out[2], along_x(1))
            near = PART_C + left * WIDE
            remote(local.at[rows(near, middle)], in_c.at[1, pl.ds(0, middle)], *out[3], along_x(NX - 1))
            return out

        def relayed(out):
            left, right, middle = (x + NX - 1) % NX, (x + 1) % NX, WIDE // 2
            more = [sems(middle) for _ in range(2)]
            settle(relay.at[0], out[0][1])
            pass_on[0] = relay[0] + local[rows(PART_C + right * WIDE, middle), :]
            remote(pass_on.at[0], in_c.at[0, pl.ds(0, middle)], *more[0], along_x(1))
            settle(relay.at[1], out[1][1])
            pass_on[1] = relay[1] + local[rows(PART_C + left * WIDE + middle, middle), :]
            remote(pass_on.at[1], in_c.at[1, pl.ds(middle, middle)], *more[1], along_x(NX - 1))
            return out[2:] + more

        if late:
            near_blocks(local, product, (0, 1, 2, 3))
            far_blocks(local, product)
            finish(local)
            yield
            by_x = opposite()
            sem_b = sems((NY - 1) * SLAB)
            scatter(axis_y, part(PART_B, SLAB), in_b, *sem_b)
        else:
            near_blocks(local, product, (2, 3))
            far_blocks(local, product)
            by_x = opposite()
            near_blocks(local, product, (1,))
            sem_b = sems((NY - 1) * SLAB)
            scatter(axis_y, part(PART_B, SLAB), in_b, *sem_b)
            near_blocks(local, product, (0,))
            finish(local)
        sem_a = sems((NZ - 1) * SLAB)
        scatter(axis_z, part(PART_A, SLAB), in_a, *sem_a)
        yield
        by_x = relayed(by_x)
        yield
        settle(in_a, sem_a[1])
        slab = total(local[rows(PART_A + z * SLAB, SLAB), :], in_a)
        for k in range(NY):
            mix_y[k, :CELL, :] = slab[k * CELL : (k + 1) * CELL]
        settle(in_b, sem_b[1])
        slab = total(local[rows(PART_B + y * SLAB, SLAB), :], in_b)
        for k in range(NZ):
            mix_z[k, :CELL, :] = slab[k * CELL : (k + 1) * CELL]
        for n, pair in enumerate(by_x):
            settle(relay.at[n % 2], pair[1])
        slab = total(local[rows(PART_C + x * WIDE, WIDE), :], in_c)
        for k in range(NY):
            mix_y[k, CELL:, :] = slab[k * THIN1 : (k + 1) * THIN1]
        for k in range(NZ):
            mix_z[k, CELL:, :] = slab[SIDE + k * THIN2 : SIDE + (k + 1) * THIN2]
        sem_y, sem_z = sems((NY - 1) * (CELL + THIN1)), sems((NZ - 1) * (CELL + THIN2))
        scatter(axis_y, lambda k: mix_y.at[k], in_y, *sem_y)
        scatter(axis_z, lambda k: mix_z.at[k], in_z, *sem_z)
        yield
        settle(in_y, sem_y[1])
        mixed = total(mix_y[y], in_y)
        in_cells[x, :CELL, :] = mixed[:CELL]
        in_thin1[z] = mixed[CELL:]
        sem_1 = sems((NZ - 1) * THIN1)
        spread(axis_z, in_thin1.at[z], *sem_1)
        settle(in_z, sem_z[1])
        mixed = total(mix_z[z], in_z)
        in_cells[x, CELL:, :] = mixed[:CELL]
        in_thin2[y] = mixed[CELL:]
        sem_2, sem_3 = sems((NY - 1) * THIN2), sems((NX - 1) * 2 * CELL)
        spread(axis_y, in_thin2.at[y], *sem_2)
        spread(axis_x, in_cells.at[x], *sem_3)
        yield
        settle(in_cells.at[pl.ds(0, NX - 1)], sem_3[1])
        both = ordered(in_cells)
        settle(in_thin1.at[pl.ds(0, NZ - 1)], sem_1[1])
        out_y[y, :CELL, :] = both[:CELL]
        out_y[y, CELL:, :] = ordered(in_thin1)
        sem_y = sems((NY - 1) * (CELL + THIN1))
        spread(axis_y, out_y.at[y], *sem_y)
        settle(in_thin2.at[pl.ds(0, NY - 1)], sem_2[1])
        out_z[z, :CELL, :] = both[CELL:]
        out_z[z, CELL:, :] = ordered(in_thin2)
        sem_z = sems((NZ - 1) * (CELL + THIN2))
        spread(axis_z, out_z.at[z], *sem_z)
        yield
        big_a, big_b = place_of(PART_A + z * SLAB, SLAB), place_of(PART_B + y * SLAB, SLAB)
        big_c = place_of(PART_C + x * WIDE, WIDE)
        settle(out_y.at[pl.ds(0, NY - 1)], sem_y[1])
        settle(out_z.at[pl.ds(0, NZ - 1)], sem_z[1])
        big_c[:SIDE, :] = out_y[:, CELL:, :].reshape(SIDE, B)
        big_c[SIDE:, :] = out_z[:, CELL:, :].reshape(WIDE - SIDE, B)
        middle = WIDE // 2
        firsts, seconds = [sems(middle) for _ in range(2)], [sems(middle) for _ in range(2)]
        upper, lower = place_of(PART_C + x * WIDE, middle), place_of(PART_C + x * WIDE + middle, middle)
        remote(upper, upper, *firsts[0], along_x(1))
        remote(lower, lower, *firsts[1], along_x(NX - 1))
        remote(lower, lower, *seconds[0], along_x(1))
        remote(upper, upper, *seconds[1], along_x(NX - 1))
        big_a[...] = out_y[:, :CELL, :].reshape(SLAB, B)
        sem_a = sems((NZ - 1) * SLAB)
        spread(axis_z, big_a, *sem_a)
        big_b[...] = out_z[:, :CELL, :].reshape(SLAB, B)
        sem_b = sems((NY - 1) * SLAB)
        spread(axis_y, big_b, *sem_b)
        yield
        forward = [sems(middle) for _ in range(2)]
        from_left = place_of(PART_C + ((x + NX - 1) % NX) * WIDE, middle)
        from_right = place_of(PART_C + ((x + 1) % NX) * WIDE + middle, middle)
        settle(from_left, firsts[0][1])
        remote(from_left, from_left, *forward[0], along_x(1))
        settle(from_right, firsts[1][1])
        remote(from_right, from_right, *forward[1], along_x(NX - 1))
        yield
        across = []
        for start, count, size, waits in (
            (PART_A, PART_B - PART_A, (NZ - 1) * SLAB, [sem_a]),
            (PART_B, PART_C - PART_B, (NY - 1) * SLAB, [sem_b]),
            (PART_C, HALF - PART_C, middle, seconds + forward),
        ):
            for _, arrived in waits:
                settle(local.at[pl.ds(0, size)], arrived)
            pair = sems(count)
            block = place_of(start, count)
            remote(block, block, *pair, sibling)
            across.append((block, pair[1]))
        yield
        for block, arrived in across:
            settle(block, arrived)
        yield
        for n, moved in enumerate(sizes):
            settle(local.at[pl.ds(0, moved)], send.at[n])
        yield

    count = len(rest) // 2
    locals_m, locals_w = rest[:count], rest[count:]
    aims = stacked(jnp.concatenate([extra[5:6, :], extra_there[5:6, :]], axis=1))

    def add_side(local):
        for c in range(NC // BLK):
            line = dot_nt(aims, dense_t[c * BLK : (c + 1) * BLK, :])
            local[BLK + c : BLK + c + 1, :BLK] = jnp.sum(line, axis=0, keepdims=True)

    job_m = job(locals_m, gathered_m, plain, add_side, False)
    job_w = job(locals_w, operator, weighted, lambda local: None, True)
    for turn in "mwmww" + "mw" * 3 + "mmwmw":
        next(job_m if turn == "m" else job_w)
    unpack(ridge, gathered_m, mat, core)
    invert_blocks(mat, inverse, 4 * core)
    next(job_m)
    unpack(ridge, gathered_m, mat, 1 - core)
    side[...] = right_side(gathered_m)

    invert_blocks(mat, inverse, 4 - 4 * core)
    advance, finish, state = first_steps(mat, inverse, columns, side[...])
    state = lax.fori_loop(0, 2, advance, state)
    next(job_w)
    state = lax.fori_loop(2, STEPS - 1, advance, state)
    value = finish(state)
    begin[...] = value
    spread_columns(value, columns)
    left[...] = side[...] - apply_full(mat, columns)
    next(job_w)
    next(job_m)
    next(job_w)


def diagonal():
    shape = (B, B)
    return lax.broadcasted_iota(jnp.int32, shape, 0) == lax.broadcasted_iota(jnp.int32, shape, 1)


def to_row(column):
    return jnp.sum(jnp.where(diagonal(), column, 0.0), axis=0, keepdims=True)


def to_column(row):
    return jnp.sum(jnp.where(diagonal(), row, 0.0), axis=1, keepdims=True)


def dot(x, y):
    return jnp.sum(jnp.sum(x * y, axis=0, keepdims=True), axis=1, keepdims=True)


def block_rows(block, column):
    return jnp.sum((block * column).reshape(B // 8, 8, B), axis=0)


def spread_columns(vector, columns):
    for j in range(NB):
        columns[j] = jnp.broadcast_to(to_column(vector[j : j + 1, :]), (B, B))


def apply_full(mat, columns):
    acc = [None] * NB
    for i in range(NB):
        column = columns[i]
        for j in range(NB):
            part = block_rows(mat[i, j], column)
            acc[j] = part if acc[j] is None else acc[j] + part
    return pack([jnp.sum(part, axis=0, keepdims=True) for part in acc])


def apply_diag(inverse, vector, columns):
    rows = []
    for b in range(NB):
        column = jnp.sum(inverse[b] * vector[b : b + 1, :], axis=1, keepdims=True)
        column = jnp.broadcast_to(column, (B, B))
        columns[b] = column
        rows.append(to_row(column))
    return pack(rows)


def invert_blocks(mat, inverse, start):
    identity = diagonal()
    one = jnp.where(identity, 1.0, 0.0)
    upper = lax.broadcasted_iota(jnp.int32, (B, B), 0) < BLK
    left = lax.broadcasted_iota(jnp.int32, (B, B), 1) < BLK
    errors, scales = [], []
    for b in range(NB // 2):
        block = jnp.where(upper == left, mat[start + b, start + b], 0.0)
        middle = jnp.where(identity, block, 0.0)
        row = lax.rsqrt(jnp.sum(middle, axis=0, keepdims=True))
        column = lax.rsqrt(jnp.sum(middle, axis=1, keepdims=True))
        block = block * row * column
        bound = jnp.max(jnp.sum(jnp.abs(block), axis=1, keepdims=True), axis=0, keepdims=True)
        errors.append(one - block / bound)
        scales.append(row * column / bound)

    def times(rows, square):
        (top, rest), (hi, lo) = split2(rows), split2(square)
        both = jnp.dot(top, hi, preferred_element_type=jnp.float32)
        both = both + jnp.dot(rest, hi, preferred_element_type=jnp.float32)
        return both + jnp.dot(top, lo, preferred_element_type=jnp.float32)

    sums = [one + error for error in errors]
    errors = [times(error, error) for error in errors]
    for n in range(DOUBLINGS):
        for b in range(NB // 2):
            if n + 1 == DOUBLINGS:
                sums[b] = sums[b] + times(sums[b], errors[b])
            else:
                both = times(jnp.concatenate([errors[b], sums[b]], axis=0), errors[b])
                errors[b] = both[:B]
                sums[b] = sums[b] + both[B:]
    for b in range(NB // 2):
        inverse[start + b] = sums[b] * scales[b]


def eliminate(mat, spare, right, columns, out):
    spare[...] = mat[...]
    spread_columns(right, columns)
    lane = lax.broadcasted_iota(jnp.int32, (B, B), 1)
    line = lax.broadcasted_iota(jnp.int32, (B, B), 0)

    def pivot(k, carry):
        kb, kr = k // B, k % B
        rows = [spare[kb, j, pl.ds(kr, 1), :] for j in range(NB)]
        entry = columns[kb, pl.ds(kr, 1), :]
        value = jnp.sum(jnp.where(lane[:1] == kr, spare[kb, kb, pl.ds(kr, 1), :], 0.0), axis=1, keepdims=True)

        def sweep(i, carry):
            factor = jnp.sum(jnp.where(lane == kr, spare[i, kb], 0.0), axis=1, keepdims=True) / value
            factor = jnp.where((line == kr) & (i == kb), 0.0, factor)
            for j in range(NB):
                spare[i, j] = spare[i, j] - factor * rows[j]
            columns[i] = columns[i] - factor * entry
            return carry

        return lax.fori_loop(0, NB, sweep, carry)

    lax.fori_loop(0, NC, pivot, 0)
    rows = []
    for b in range(NB):
        scale = jnp.sum(jnp.where(diagonal(), spare[b, b], 0.0), axis=1, keepdims=True)
        rows.append(to_row(columns[b] / scale))
    out[...] = pack(rows)


def first_steps(mat, inverse, columns, right):
    zero = jnp.zeros((NB, B), jnp.float32)
    pre = apply_diag(inverse, right, columns)
    size = dot(right, pre)
    bound = (TOL * TOL) * size
    image = apply_full(mat, columns)

    def advance(_, carry):
        res, pre, image, step, moved, total, size, ratio, length = carry
        step = pre + ratio * step
        moved = image + ratio * moved
        total = total + length * step
        res = res - length * moved
        pre = apply_diag(inverse, res, columns)
        latest = dot(res, pre)
        image = apply_full(mat, columns)
        active = latest > bound
        ratio = jnp.where(active, latest / size, 0.0)
        further = jnp.where(active, latest / (dot(image, pre) - ratio * latest / length), 0.0)
        return res, pre, image, step, moved, total, latest, ratio, further

    def finish(carry):
        _, pre, _, step, _, total, _, ratio, length = carry
        return total + length * (pre + ratio * step)

    start = (right, pre, image, zero, zero, zero, size, jnp.zeros((1, 1), jnp.float32), size / dot(image, pre))
    return advance, finish, start


def solve(mat, inverse, spare, columns, right, out, given=None, least=0.0):
    zero = jnp.zeros((NB, B), jnp.float32)

    def inner(res, pre, size, bound):
        image = apply_full(mat, columns)

        def going(carry):
            return (carry[0] < LIMIT) & (carry[1] > bound)

        def advance(carry):
            count, _, res, pre, image, step, moved, total, size, ratio, length = carry
            step = pre + ratio * step
            moved = image + ratio * moved
            total = total + length * step
            res = res - length * moved
            pre = apply_diag(inverse, res, columns)
            latest = dot(res, pre)
            image = apply_full(mat, columns)
            ratio = latest / size
            length = latest / (dot(image, pre) - ratio * latest / length)
            return count + 1, latest[0, 0], res, pre, image, step, moved, total, latest, ratio, length

        start = (
            jnp.int32(0), size[0, 0], res, pre, image, zero, zero, zero,
            size, jnp.zeros((1, 1), jnp.float32), size / dot(image, pre),
        )
        return lax.while_loop(going, advance, start)[7]

    def residual(value):
        spread_columns(value, columns)
        res = right - apply_full(mat, columns)
        pre = apply_diag(inverse, res, columns)
        return res, pre, dot(res, pre)

    pre = apply_diag(inverse, right, columns)
    whole = dot(right, pre)
    first = jnp.maximum(whole[0, 0], least)
    if given is None:
        out[...] = zero
        begun = (jnp.int32(0), whole[0, 0], right, pre, whole)
    else:
        out[...], res = given
        pre = apply_diag(inverse, res, columns)
        size = dot(res, pre)
        begun = (jnp.int32(0), size[0, 0], res, pre, size)

    def unsolved(carry):
        return (carry[0] < ROUNDS) & (carry[1] > CHECK * CHECK * first)

    def improve(carry):
        count, _, res, pre, size = carry
        out[...] += inner(res, pre, size, TOL * TOL * first)
        res, pre, size = residual(out[...])
        return count + 1, size[0, 0], res, pre, size

    final = lax.while_loop(unsolved, improve, begun)[1]

    @pl.when(jnp.logical_not(final <= CHECK * CHECK * first))
    def _():
        eliminate(mat, spare, right, columns, out)

    return first


def corner_fixed(block):
    low = lax.broadcasted_iota(jnp.int32, (B, B), 0) >= BLK
    low = low & (lax.broadcasted_iota(jnp.int32, (B, B), 1) < BLK)
    return jnp.where(low, block.T, block)


def right_side(grams):
    left = lax.broadcasted_iota(jnp.int32, (1, B), 1) < BLK
    sides = []
    for j in range(NB):
        even = grams[BLK + 2 * j : BLK + 2 * j + 1, :]
        odd = grams[BLK + 2 * j + 1 : BLK + 2 * j + 2, :]
        sides.append(jnp.where(left, even, pltpu.roll(odd, BLK, 1)))
    return pack(sides)


def unpack(ridge, grams, mat, core):
    identity = diagonal()
    for n in range(PER_CORE):
        block = grams[pl.ds(pl.multiple_of(core * HALF + n * B, B), B), :]
        if n == 0:
            block = corner_fixed(block)
        if n < 16:
            i, d = 4 * core + n // 4, n % 4
        else:
            i, d = 6 * core + n - 16, 4
        j = (i + d) % NB
        if d == 0:
            mat[i, i] = block + jnp.where(identity, ridge, 0.0)
        else:
            mat[i, j] = block
            mat[j, i] = block.T


def apply_weighted(blocks, vector, columns):
    down = [jnp.zeros((8, B), jnp.float32)] * NB
    rows = []
    for i in range(NB):
        column = columns[i]
        across = jnp.zeros((B, B), jnp.float32)
        for j in range(NB):
            if (i, j) in INDEX:
                block = blocks[INDEX[i, j]]
                down[j] = down[j] + block_rows(block, column)
                if j != i:
                    across = across + block * vector[j : j + 1, :]
        rows.append(to_row(jnp.sum(across, axis=1, keepdims=True)))
    return pack([jnp.sum(part, axis=0, keepdims=True) + row for part, row in zip(down, rows)])


def weighted_square(blocks, vector, columns):
    total = jnp.zeros((8, B), jnp.float32)
    twice = 2.0 * vector
    for i in range(NB):
        across = jnp.zeros((B, B), jnp.float32)
        for j in range(NB):
            if (i, j) in INDEX:
                row = vector if i == j else twice
                across = across + blocks[INDEX[i, j]] * row[j : j + 1, :]
        total = total + block_rows(across, columns[i])
    return jnp.sum(jnp.sum(total, axis=0, keepdims=True), axis=1, keepdims=True)


def design_lines(dense_t, columns):
    lines = []
    for half in range(2):
        acc = jnp.zeros((8, B), jnp.float32)
        for j in range(NB):
            part = dense_t[j * B : (j + 1) * B, half * B : (half + 1) * B].astype(jnp.float32)
            acc = acc + block_rows(part, columns[j])
        lines.append(jnp.sum(acc, axis=0, keepdims=True))
    return lines


def solver_kernel(
    ridge, blocks, dense_t, mat, inverse, side, begin, left, solution, fitted, spare, columns, first, second
):
    g = side[...]
    least = solve(mat, inverse, spare, columns, g, first, (begin[...], left[...]))
    z = first[...]
    spread_columns(z, columns)
    h = apply_weighted(blocks, z, columns) + ridge * z
    first_lines = design_lines(dense_t, columns)
    gain = dot(g, z)
    length = gain / dot(z, h)
    rest = g - length * h
    solve(mat, inverse, spare, columns, rest, second, least=least)
    s = second[...]
    latest = dot(rest, s)
    step = s + (latest / gain) * z
    spread_columns(step, columns)
    curve = weighted_square(blocks, step, columns) + ridge * dot(step, step)
    last_lines = design_lines(dense_t, columns)
    further = jnp.where(curve > 0.0, latest / curve, 0.0)
    solution[...] = length * z + further * step
    for half in range(2):
        fitted[half : half + 1, :] = length * first_lines[half] + further * last_lines[half]


def space(*shape):
    return pltpu.VMEM(shape, jnp.float32)


def shaped(*shape):
    return jax.ShapeDtypeStruct(shape, jnp.float32)


WHOLE = pl.BlockSpec(memory_space=pltpu.VMEM)
LIMITS = dict(vmem_limit_bytes=32 << 20)


def body(values, pattern, targets, root_weights):
    tiles = values.shape[0]
    own_rows = tiles * BLK
    rows_total = own_rows * lax.axis_size("rows") * lax.axis_size("grp")
    ridge = rows_total / (2.0 * NC)
    groups = 8 + 2 + 3 + 2 + 8 + 3
    job_space = [
        space(HALF, B),
        space(NZ - 1, SLAB, B),
        space(NY - 1, SLAB, B),
        space(2, WIDE, B),
        space(2, WIDE // 2, B),
        space(2, WIDE // 2, B),
        space(NY, CELL + THIN1, B),
        space(NZ, CELL + THIN2, B),
        space(NY - 1, CELL + THIN1, B),
        space(NZ - 1, CELL + THIN2, B),
        space(NX, 2 * CELL, B),
        space(NZ, THIN1, B),
        space(NY, THIN2, B),
        space(NY, CELL + THIN1, B),
        space(NZ, CELL + THIN2, B),
    ] + [pltpu.SemaphoreType.DMA((groups,))] * 2
    operator, dense_t, mat, inverse, side, begin, left = pl.pallas_call(
        lambda *refs: reduce_kernel(ridge, *refs),
        out_shape=(
            shaped(2 * HALF, B),
            jax.ShapeDtypeStruct((NC, own_rows), jnp.bfloat16),
            shaped(NB, NB, B, B),
            shaped(NB, B, B),
            shaped(NB, B),
            shaped(NB, B),
            shaped(NB, B),
        ),
        in_specs=[pl.BlockSpec(memory_space=pltpu.HBM)] * 4,
        out_specs=(WHOLE,) * 7,
        scratch_shapes=[
            pltpu.VMEM((2, B, WIDTH), jnp.bfloat16),
            pltpu.VMEM(pattern.shape, jnp.int32),
            space(1, WIDTH),
            space(1, WIDTH),
            space(2, B, WIDTH),
            space(8, WIDTH),
            space(2, B, WIDTH),
            space(8, WIDTH),
            pltpu.VMEM((NC + NC // 2, 2 * WIDTH), jnp.bfloat16),
            space(2 * HALF, B),
            space(NB, B, B),
            pltpu.SemaphoreType.DMA((4,)),
            pltpu.SemaphoreType.DMA((2,)),
            pltpu.SemaphoreType.DMA((2,)),
        ]
        + job_space * 2,
        compiler_params=pltpu.CompilerParams(collective_id=0, has_side_effects=True, **LIMITS),
    )(
        *(
            pltpu.with_memory_space_constraint(operand, pltpu.HBM)
            for operand in (
                values.reshape(tiles // 2, 2 * BLK, WIDTH), pattern, targets.reshape(1, -1), root_weights.reshape(1, -1)
            )
        )
    )
    solution_rows, fitted = pl.pallas_call(
        lambda *refs: solver_kernel(ridge, *refs),
        out_shape=(shaped(NB, B), shaped(own_rows // B, B)),
        in_specs=[WHOLE] * 7,
        out_specs=(WHOLE,) * 2,
        scratch_shapes=[space(NB, NB, B, B), space(NB, B, B), space(NB, B), space(NB, B)],
        compiler_params=pltpu.CompilerParams(**LIMITS),
    )(operator.reshape(len(PAIRS), B, B), dense_t, mat, inverse, side, begin, left)
    return solution_rows.reshape(-1), fitted.reshape(-1)


def solution(mesh):
    in_specs = (
        P(("rows", "grp"), None, None),
        P(("rows", "grp"), None),
        P(("rows", "grp")),
        P(("rows", "grp")),
    )
    out_specs = (P(), P(("rows", "grp")))
    return jax.shard_map(body, mesh=mesh, in_specs=in_specs, out_specs=out_specs, check_vma=False)
```
